256 devices in a mesh: ctx: 32 (over z, x_lo, core), head: 8 (over y, x_hi).
Axes of the slice: x: 4 (x_hi: 2, x_lo: 2; x = x_hi * 2 + x_lo), y: 4, z: 8, core: 2. Of those that a mesh axis runs over, the one named last changes fastest.
Arguments:
- queries: bfloat16 [4096, 12288], P('ctx', 'head'), may hold values from -8 to 8
- compressed: bfloat16 [4096, 576], P('ctx'), may hold values from -16 to 16
- latent_gain: float32 [512], replicated, may hold values from 0.25 to 1.75
- w_uk: bfloat16 [512, 8192], P(None, 'head'), may hold values from -0.25 to 0.25
- w_uv: bfloat16 [512, 8192], P(None, 'head'), may hold values from -0.25 to 0.25
- w_out: bfloat16 [8192, 7168], P('head', 'ctx'), may hold values from -0.5 to 0.5
Outputs:
- output: bfloat16 [4096, 7168], P('ctx', 'head')
The draws below stay inside these ranges and needn't reach their ends.
All inputs are finite; a program needn't handle non-finite values.
Results may differ from the reference program's by a relative error of at most 0.018.
Values may be sent and summed in bfloat16 or wider, within the bound.
A program may use at most 64 MiB of HBM per device.

```python
import jax
import jax.numpy as jnp
from jax import lax

D = 7168
H = 64
LATENT = 512
ROPE = 64
NOPE = 128
TOKENS = 4096


def draw_queries(key, part):
    key = jax.random.fold_in(key, 1)
    base = jnp.clip(jax.random.normal(key, (TOKENS, H * (NOPE + ROPE)), jnp.float32), -4.0, 4.0)
    return base.astype(jnp.bfloat16)


def draw_compressed(key, part):
    key = jax.random.fold_in(key, 2)
    result = jnp.clip(jax.random.normal(key, (TOKENS, LATENT + ROPE), jnp.float32), -4.0, 4.0)
    return result.astype(jnp.bfloat16)


def level_of(rng, dims, shards, low, top_value):
    def one(axis_at, blocks):
        draws = jax.random.uniform(jax.random.fold_in(jax.random.fold_in(rng, 6), axis_at), (blocks,), jnp.float32, low / len(shards), top_value / len(shards))
        return jnp.repeat(jnp.exp(draws), dims[axis_at] // blocks).reshape((-1,) + (1,) * (len(dims) - axis_at - 1))

    factor_of = one(*shards[0])
    for cut in shards[1:]:
        factor_of = factor_of * one(*cut)
    return factor_of


def gaussian(own_key, extent, width, limit, cuts=(), kind=jnp.bfloat16):
    entries = width * jax.random.normal(own_key, extent, jnp.float32)
    if cuts:
        entries = entries * level_of(own_key, extent, cuts, -0.22, 0.18)
    return jnp.clip(entries, -limit, limit).astype(kind)


def setup_inputs(seed: int = 0) -> dict:
    key_list = jax.random.split(jax.random.key(seed), 7)
    queries = draw_queries(jax.random.fold_in(key_list[6], 71), 0)
    compressed = draw_compressed(jax.random.fold_in(key_list[6], 71), 0)
    latent_gain = jnp.clip(1.0 + 0.15 * jax.random.normal(key_list[2], (LATENT,), jnp.float32), 0.25, 1.75)
    w_uk = gaussian(key_list[3], (LATENT, H * NOPE), LATENT ** -0.5, 0.25, ((1, 8),))
    w_uv = gaussian(key_list[4], (LATENT, H * NOPE), LATENT ** -0.5, 0.25, ((1, 8),))
    w_out = gaussian(key_list[5], (H * NOPE, D), NOPE ** -0.5, 0.5, ((0, 8), (1, 32)))
    return dict(queries=queries, compressed=compressed, latent_gain=latent_gain, w_uk=w_uk, w_uv=w_uv, w_out=w_out)


def compress_norm(compressed, latent_gain):
    latent = compressed[:, :LATENT].astype(jnp.float32)
    mean_square = lax.optimization_barrier(jnp.mean(latent * latent, axis=1, keepdims=True))
    normed = (latent * lax.rsqrt(mean_square + 1e-06) * latent_gain).astype(jnp.bfloat16)
    return normed

def reference(queries, compressed, latent_gain, w_uk, w_uv, w_out):
    normed = compress_norm(compressed, latent_gain)
    keys_content = jnp.dot(normed, w_uk, preferred_element_type=jnp.float32).astype(jnp.bfloat16)
    values = jnp.dot(normed, w_uv, preferred_element_type=jnp.float32).astype(jnp.bfloat16)
    keys_rotary = compressed[:, LATENT:]
    position = jnp.arange(TOKENS, dtype=jnp.int32)
    visible = position[:, None] >= position[None, :]

    def one_head(head_index):
        query_head = lax.dynamic_slice_in_dim(queries, head_index * (NOPE + ROPE), NOPE + ROPE, 1)
        key_head = lax.dynamic_slice_in_dim(keys_content, head_index * NOPE, NOPE, 1)
        value_head = lax.dynamic_slice_in_dim(values, head_index * NOPE, NOPE, 1)
        scores = jnp.dot(query_head[:, :NOPE], key_head.T, preferred_element_type=jnp.float32)
        scores = scores + jnp.dot(query_head[:, NOPE:], keys_rotary.T, preferred_element_type=jnp.float32)
        scores = scores * (NOPE + ROPE) ** (-0.5)
        scores = jnp.where(visible, scores, -jnp.inf)
        row_max = lax.optimization_barrier(jnp.max(scores, axis=1, keepdims=True))
        probabilities = jnp.exp(scores - row_max)
        weight_sum = lax.optimization_barrier(jnp.sum(probabilities, axis=1, keepdims=True))
        rounded_weights = probabilities.astype(jnp.bfloat16)
        return jnp.dot(rounded_weights, value_head, preferred_element_type=jnp.float32) / weight_sum
    per_head = lax.map(one_head, jnp.arange(H, dtype=jnp.int32))
    attention = jnp.transpose(per_head, (1, 0, 2)).reshape(TOKENS, H * NOPE).astype(jnp.bfloat16)
    return jnp.dot(attention, w_out, preferred_element_type=jnp.float32).astype(jnp.bfloat16)
```

```python
import functools
import math

import jax
import jax.numpy as jnp
from jax import lax
from jax.experimental import pallas as pl
from jax.experimental.pallas import tpu as pltpu
from jax.sharding import PartitionSpec as P

LATENT = 512
ROPE = 64
NOPE = 128
HD = NOPE + ROPE
SCALE = HD ** -0.5 * math.log2(math.e)
NT = (((1,), (1,)), ((), ()))


def attention_kernel(q_ref, lat_ref, uk_ref, uv_ref, out_ref, qc_ref, qr_ref, m_ref, l_ref, acc_ref):
    rows = q_ref.shape[0]
    heads = uk_ref.shape[1] // NOPE
    total = rows * heads
    block = 512
    chunk = 256
    me = lax.axis_index("ctx")
    first = me * rows
    z = first // block
    for h in range(heads):
        qh = q_ref[:, h * HD:h * HD + NOPE]
        qa = lax.dot_general(qh, uk_ref[:, h * NOPE:(h + 1) * NOPE], NT, preferred_element_type=jnp.float32)
        qc_ref[h * rows:(h + 1) * rows, :] = (qa * SCALE).astype(jnp.bfloat16)
        qr = q_ref[:, h * HD + NOPE:(h + 1) * HD].astype(jnp.float32)
        qr_ref[h * rows:(h + 1) * rows, :] = (qr * SCALE).astype(jnp.bfloat16)

    def visit(at, masked):
        start = pl.multiple_of(at * block, block)
        lat = lat_ref[pl.ds(start, block), :LATENT]
        rot = lat_ref[pl.ds(start, block), LATENT:]
        for r in range(0, total, chunk):
            s = lax.dot_general(qc_ref[r:r + chunk, :], lat, NT, preferred_element_type=jnp.float32)
            s = s + lax.dot_general(qr_ref[r:r + chunk, :], rot, NT, preferred_element_type=jnp.float32)
            if masked:
                row = first - start + lax.rem(lax.broadcasted_iota(jnp.int32, s.shape, 0), rows)
                s = jnp.where(row >= lax.broadcasted_iota(jnp.int32, s.shape, 1), s, -jnp.inf)
                m_new = jnp.max(s, axis=1, keepdims=True)
                p = jnp.exp2(s - m_new)
                l_ref[r:r + chunk, :] = jnp.sum(p, axis=1, keepdims=True)
                acc_ref[r:r + chunk, :] = jnp.dot(p.astype(jnp.bfloat16), lat, preferred_element_type=jnp.float32)
            else:
                m_old = m_ref[r:r + chunk, :]
                m_new = jnp.maximum(m_old, jnp.max(s, axis=1, keepdims=True))
                alpha = jnp.exp2(m_old - m_new)
                p = jnp.exp2(s - m_new)
                l_ref[r:r + chunk, :] = l_ref[r:r + chunk, :] * alpha + jnp.sum(p, axis=1, keepdims=True)
                acc_ref[r:r + chunk, :] = acc_ref[r:r + chunk, :] * alpha + jnp.dot(
                    p.astype(jnp.bfloat16), lat, preferred_element_type=jnp.float32)
            m_ref[r:r + chunk, :] = m_new

    visit(z, True)

    @pl.loop(0, z)
    def _(at):
        visit(at, False)

    for h in range(heads):
        o = acc_ref[h * rows:(h + 1) * rows, :] / l_ref[h * rows:(h + 1) * rows, :]
        a = jnp.dot(o.astype(jnp.bfloat16), uv_ref[:, h * NOPE:(h + 1) * NOPE], preferred_element_type=jnp.float32)
        out_ref[:, h * NOPE:(h + 1) * NOPE] = a.astype(jnp.bfloat16)


def compress_norm(compressed, latent_gain):
    latent = compressed[:, :LATENT].astype(jnp.float32)
    mean_square = jnp.mean(latent * latent, axis=1, keepdims=True)
    normed = (latent * lax.rsqrt(mean_square + 1e-06) * latent_gain).astype(jnp.bfloat16)
    return jnp.concatenate([normed, compressed[:, LATENT:]], axis=1)


def on_device(queries, compressed, latent_gain, w_uk, w_uv, w_out):
    rows = queries.shape[0]
    heads = w_uk.shape[1] // NOPE
    ctx = lax.axis_size("ctx")
    along_z = [[j + 4 * z for z in range(ctx // 4)] for j in range(4)]
    within = [[4 * z + j for j in range(4)] for z in range(ctx // 4)]
    latents = lax.all_gather(compress_norm(compressed, latent_gain), "ctx", axis=0, tiled=True)
    w_all = lax.all_gather(w_out, "ctx", axis=0, tiled=False, axis_index_groups=along_z)
    attention = pl.pallas_call(
        attention_kernel,
        out_shape=jax.ShapeDtypeStruct((rows, heads * NOPE), jnp.bfloat16),
        in_specs=[pl.BlockSpec(memory_space=pltpu.VMEM)] * 4,
        out_specs=pl.BlockSpec(memory_space=pltpu.VMEM),
        scratch_shapes=[
            pltpu.VMEM((rows * heads, LATENT), jnp.bfloat16),
            pltpu.VMEM((rows * heads, ROPE), jnp.bfloat16),
            pltpu.VMEM((rows * heads, 1), jnp.float32),
            pltpu.VMEM((rows * heads, 1), jnp.float32),
            pltpu.VMEM((rows * heads, LATENT), jnp.float32),
        ],
        compiler_params=pltpu.CompilerParams(vmem_limit_bytes=48 * 1024 * 1024),
        name="attention",
    )(queries, latents, w_uk, w_uv)
    strip = lax.all_gather(attention, "ctx", axis=0, tiled=True, axis_index_groups=within)
    partial = jnp.einsum("tk,zkn->ztn", strip, w_all, preferred_element_type=jnp.float32).astype(jnp.bfloat16)
    mine = lax.psum_scatter(partial, "head", scatter_dimension=0, tiled=False)
    mine = mine.reshape(4, rows, mine.shape[1])
    swapped = lax.all_to_all(mine, "ctx", 0, 0, axis_index_groups=within, tiled=True)
    return jnp.transpose(swapped, (1, 0, 2)).reshape(rows, -1)


def solution(mesh):
    return jax.shard_map(
        on_device,
        mesh=mesh,
        in_specs=(
            P("ctx", "head"),
            P("ctx", None),
            P(),
            P(None, "head"),
            P(None, "head"),
            P("head", "ctx"),
        ),
        out_specs=P("ctx", "head"),
        check_vma=False,
    )
```

```python
import math

import jax
import jax.numpy as jnp
from jax import lax
from jax.experimental import pallas as pl
from jax.experimental.pallas import tpu as pltpu
from jax.sharding import PartitionSpec as P

LATENT = 512
ROPE = 64
NOPE = 128
HD = NOPE + ROPE
WIDE = 640
ROWS = 128
HEADS = 8
STRIP = 4 * ROWS
TOTAL = HEADS * ROWS
CHUNK = 512
HALF = 112
NZ = 8
SCALE = HD ** -0.5 * math.log2(math.e)
NT = (((1,), (1,)), ((), ()))
MESH = pl.DeviceIdType.MESH


def al(value, unit):
    return pl.multiple_of(value, unit)


def kernel(q_ref, comp_ref, gain_ref, uk_ref, uv_ref, w_ref, out_ref,
           lat, ball, qt, uvt, m_ref, l_ref, acc, abuf, cbuf, rbuf, fsrc, fin,
           s1s, s1r, s2s, s2r, s3s, s3r, s4s, s4r, brs, brr, bls, blr,
           axs, axr, acs, acr, afs, afr, cs, cr, fs, fr):
    ctx = lax.axis_index("ctx")
    head = lax.axis_index("head")
    z = ctx // 4
    j = ctx % 4
    y = head // 2
    xh = head % 2
    xl = j // 2
    base = 4 * z
    sib = j + 1 - 2 * (j % 2)
    opp = (j + 2) % 4
    opp_sib = (sib + 2) % 4
    x_lo = (base + opp, head)
    core = (base + sib, head)
    x_up = (base + opp, 2 * y + (xh + xl) % 2)
    x_down = (base + opp, 2 * y + (xh + xl + 1) % 2)
    z_up = (4 * ((z + 1) % NZ) + j, head)
    z_down = (4 * ((z + 7) % NZ) + j, head)

    def copy(src, dst, send, recv, device):
        return pltpu.make_async_remote_copy(
            src_ref=src, dst_ref=dst, send_sem=send, recv_sem=recv, device_id=device, device_id_type=MESH)

    def arrived(dst, recv):
        copy(dst, dst, recv, recv, core).wait_recv()

    def left(src, send):
        copy(src, src, send, send, core).wait_send()

    barrier = pltpu.get_barrier_semaphore()

    def greet(device):
        pl.semaphore_signal(barrier, inc=1, device_id=device, device_id_type=MESH)

    for k in range(1, NZ):
        greet((4 * ((z + k) % NZ) + j, head))
    for k in range(1, HEADS):
        greet((ctx, (head + k) % HEADS))
    greet(x_up)
    greet(x_down)
    greet(core)
    for p in range(4):
        for b in range(2):
            @pl.when((p != j) | (j != y) | (b != xh))
            def _():
                greet((base + p, 2 * j + b))

    own = comp_ref[:, :LATENT].astype(jnp.float32)
    mean_square = jnp.mean(own * own, axis=1, keepdims=True)
    normed = (own * lax.rsqrt(mean_square + 1e-06) * gain_ref[...]).astype(jnp.bfloat16)
    mine = pl.ds(al(j * ROWS, ROWS), ROWS)
    lat[z, mine, :LATENT] = normed
    lat[z, mine, LATENT:] = jnp.concatenate(
        [comp_ref[:, LATENT:], jnp.zeros((ROWS, WIDE - LATENT - ROPE), jnp.bfloat16)], axis=1)
    wt = w_ref[...].T
    ball[z, 0] = wt[:HALF]
    ball[z, 1] = wt[HALF:]

    pl.semaphore_wait(barrier, jnp.where(j == y, 24, 25))

    def rows_of(zs, member, start, count):
        return lat.at[zs, pl.ds(al(member * ROWS + start, 16), count), :]

    def z_copy(k):
        part = rows_of(z, j, y * 32, 32)
        return copy(part, part, s1s.at[k], s1r.at[z], (4 * (z + k) + j, head))

    for k in range(1, NZ):
        @pl.when(z + k < NZ)
        def _():
            z_copy(k).start()

    def y_copy(zs, k):
        part = rows_of(zs, j, y * 32, 32)
        return copy(part, part, s2s.at[zs, k - 1], s2r.at[zs, k - 1], (ctx, 2 * ((y + k) % 4) + xh))

    def x_copies(zs):
        low = rows_of(zs, j, 0, 64)
        high = rows_of(zs, j, 64, 64)
        return (copy(low, low, s3s.at[zs, 0], s3r.at[zs, 0], x_up),
                copy(high, high, s3s.at[zs, 1], s3r.at[zs, 1], x_down))

    def core_copy(zs, member, slot):
        part = rows_of(zs, member, 0, ROWS)
        return copy(part, part, s4s.at[zs, slot], s4r.at[zs, slot], core)

    def stage1(d):
        zs = z - d
        arrived(rows_of(zs, j, y * 32, 32), s1r.at[zs])
        for k in range(1, 4):
            y_copy(zs, k).start()

    def stage2(d, wait=True):
        zs = z - d
        if wait:
            for k in range(1, 4):
                arrived(rows_of(zs, j, ((y + 4 - k) % 4) * 32, 32), s2r.at[zs, k - 1])
        for each in x_copies(zs):
            each.start()
        core_copy(zs, j, 0).start()

    def stage3(d):
        zs = z - d
        arrived(rows_of(zs, opp, 0, 64), s3r.at[zs, 0])
        arrived(rows_of(zs, opp, 64, 64), s3r.at[zs, 1])
        core_copy(zs, opp, 1).start()

    def stage4(d):
        zs = z - d
        arrived(rows_of(zs, sib, 0, ROWS), s4r.at[zs, 0])
        arrived(rows_of(zs, opp_sib, 0, ROWS), s4r.at[zs, 1])

    def ring_up(u):
        part = ball.at[(z + NZ - u // 2) % NZ, u % 2]
        return copy(part, part, brs.at[u], brr.at[u], z_up)

    def ring_down(u):
        part = ball.at[(z + u // 2) % NZ, 1 - u % 2]
        return copy(part, part, bls.at[u], blr.at[u], z_down)

    def ring_arrived(k):
        arrived(ball.at[(z + 7 - k // 2) % NZ, k % 2], brr.at[k])
        arrived(ball.at[(z + 1 + k // 2) % NZ, 1 - k % 2], blr.at[k])

    def forward(k):
        ring_arrived(k)

        @pl.when(k < 5)
        def _():
            ring_up(k + 2).start()
            ring_down(k + 2).start()

    def when_in(d, act):
        @pl.when(d <= z)
        def _():
            act(d)

    stage2(0, wait=False)
    for u in range(2):
        ring_up(u).start()
        ring_down(u).start()

    def absorb(h):
        lanes = slice(h * ROWS, (h + 1) * ROWS)
        qa = lax.dot_general(uk_ref[:, h * NOPE:(h + 1) * NOPE], q_ref[:, h * HD:h * HD + NOPE], NT,
                             preferred_element_type=jnp.float32)
        qt[:LATENT, lanes] = (qa * SCALE).astype(jnp.bfloat16)
        qr = q_ref[:, h * HD + NOPE:(h + 1) * HD].astype(jnp.float32) * SCALE
        qt[LATENT:LATENT + ROPE, lanes] = qr.T.astype(jnp.bfloat16)

    qt[LATENT + ROPE:, :] = jnp.zeros((WIDE - LATENT - ROPE, TOTAL), jnp.bfloat16)
    for h in range(HEADS):
        absorb(h)
    when_in(1, stage1)
    when_in(2, stage1)
    uvt[...] = uv_ref[...].T

    def visit(zs, first):
        block = lat[zs]
        turned = block[:, :LATENT].T

        def score(c):
            s = jnp.dot(block, qt[:, c * CHUNK:(c + 1) * CHUNK], preferred_element_type=jnp.float32)
            if first:
                row = j * ROWS + lax.broadcasted_iota(jnp.int32, s.shape, 1) % ROWS
                s = jnp.where(row >= lax.broadcasted_iota(jnp.int32, s.shape, 0), s, -jnp.inf)
            return s

        def rest(s, c):
            lanes = slice(c * CHUNK, (c + 1) * CHUNK)
            m_new = jnp.max(s, axis=0, keepdims=True)
            if not first:
                m_old = m_ref[:, lanes]
                m_new = jnp.maximum(m_old, m_new)
                alpha = jnp.exp2(m_old - m_new)
            p = jnp.exp2(s - m_new)
            total = jnp.sum(p, axis=0, keepdims=True)
            part = jnp.dot(turned, p.astype(jnp.bfloat16), preferred_element_type=jnp.float32)
            m_ref[:, lanes] = m_new
            if first:
                l_ref[:, lanes] = total
                acc[:, lanes] = part
            else:
                l_ref[:, lanes] = l_ref[:, lanes] * alpha + total
                acc[:, lanes] = acc[:, lanes] * alpha + part

        s = score(0)
        later = score(1)
        rest(s, 0)
        rest(later, 1)

    when_in(1, stage2)
    stage3(0)
    when_in(3, stage1)
    when_in(2, stage2)
    when_in(1, stage3)
    stage4(0)
    visit(z, True)

    @pl.loop(1, z + 1)
    def _(i):
        when_in(i + 3, stage1)
        when_in(i + 2, stage2)
        when_in(i + 1, stage3)
        stage4(i)
        visit(z - i, False)

        @pl.when(i % 2 == 0)
        def _():
            forward(i // 2 - 1)

    done = z // 2

    def piece(member, c):
        return abuf.at[pl.ds(c * CHUNK, CHUNK), pl.ds(al(member * ROWS, ROWS), ROWS)]

    def a_x(c):
        return copy(piece(j, c), piece(j, c), axs.at[c], axr.at[c], x_lo)

    def a_core(c):
        return copy(piece(j, c), piece(j, c), acs.at[c], acr.at[c], core)

    def a_forward(c):
        return copy(piece(opp, c), piece(opp, c), afs.at[c], afr.at[c], core)

    for c in range(2):
        for h in range(c * 4, c * 4 + 4):
            lanes = slice(h * ROWS, (h + 1) * ROWS)
            o = (acc[:, lanes] / l_ref[:, lanes]).astype(jnp.bfloat16)
            a = jnp.dot(uvt[h * NOPE:(h + 1) * NOPE, :], o, preferred_element_type=jnp.float32)
            abuf[h * NOPE:(h + 1) * NOPE, mine] = a.astype(jnp.bfloat16)
        a_x(c).start()
        a_core(c).start()
    for c in range(2):
        arrived(piece(opp, c), axr.at[c])
        a_forward(c).start()
    for c in range(2):
        arrived(piece(sib, c), acr.at[c])
    for c in range(2):
        arrived(piece(opp_sib, c), afr.at[c])

    def places(s):
        u = jnp.maximum(s - 1, 0)
        far = (s + 1) // 2
        up = (z + NZ - far) % NZ
        down = (z + far) % NZ
        return up, down, u % 2

    def c_copy(s, r, t, b):
        return copy(cbuf.at[s, r, t], rbuf.at[s, head], cs.at[s, r, t], cr.at[s, head], (ctx, 2 * t + b))

    def each_copy(s, act):
        odd = places(s)[2]
        for r in range(2):
            b = (odd + r) % 2
            for t in range(4):
                @pl.when((t != y) | (b != xh))
                def _():
                    act(c_copy(s, r, t, b))

    def multiply(s):
        up, down, odd = places(s)
        both = jnp.concatenate([ball[up, odd], ball[down, 1 - odd]], axis=0)
        ct = jnp.dot(both, abuf[...], preferred_element_type=jnp.float32).astype(jnp.bfloat16)
        for r in range(2):
            for t in range(4):
                cbuf[s, r, t] = ct[r * HALF:(r + 1) * HALF, t * ROWS:(t + 1) * ROWS]
        each_copy(s, lambda each: each.start())

    def home(s):
        up, down, odd = places(s)
        same = (odd + xh) % 2
        return up * (1 - same) + down * same, same

    spot = fin.at[pl.ds(al((2 * j + xh) * HALF, HALF), HALF), :]

    def f_copy(s):
        n, _ = home(s)
        return copy(fsrc.at[s], spot, fs.at[s], fr.at[2 * j + xh], (base + y, n))

    def is_here(s):
        return (y == j) & (home(s)[0] == head)

    def gather(s):
        n, r = home(s)
        for k in range(1, HEADS):
            peer = (head + k) % HEADS
            arrived(rbuf.at[s, peer], cr.at[s, peer])
        total = cbuf[s, r, y].astype(jnp.float32)
        for k in range(1, HEADS):
            total = total + rbuf[s, (head + k) % HEADS].astype(jnp.float32)
        fsrc[s] = total.astype(jnp.bfloat16)
        here = is_here(s)

        @pl.when(here)
        def _():
            spot[...] = fsrc[s]

        @pl.when(jnp.logical_not(here))
        def _():
            f_copy(s).start()

    @pl.loop(0, NZ)
    def _(s):
        @pl.when(s - 1 >= done)
        def _():
            forward(s - 1)

        multiply(s)

        @pl.when(s >= 2)
        def _():
            gather(s - 2)

    gather(6)
    gather(7)

    for p in range(4):
        for b in range(2):
            @pl.when((p != j) | (j != y) | (b != xh))
            def _():
                arrived(fin.at[pl.ds((2 * p + b) * HALF, HALF), :], fr.at[2 * p + b])
    out_ref[...] = fin[...].T

    for k in range(1, NZ):
        @pl.when(z + k < NZ)
        def _():
            z_copy(k).wait_send()

    @pl.loop(0, z + 1)
    def _(zs):
        @pl.when(zs < z)
        def _():
            for k in range(1, 4):
                y_copy(zs, k).wait_send()
        for each in x_copies(zs):
            each.wait_send()
        core_copy(zs, j, 0).wait_send()
        core_copy(zs, opp, 1).wait_send()

    @pl.loop(0, 7)
    def _(u):
        ring_up(u).wait_send()
        ring_down(u).wait_send()

    for c in range(2):
        a_x(c).wait_send()
        a_core(c).wait_send()
        a_forward(c).wait_send()

    @pl.loop(0, NZ)
    def _(s):
        each_copy(s, lambda each: each.wait_send())

        @pl.when(jnp.logical_not(is_here(s)))
        def _():
            f_copy(s).wait_send()


def on_device(queries, compressed, latent_gain, w_uk, w_uv, w_out):
    dma = pltpu.SemaphoreType.DMA
    bf = jnp.bfloat16
    return pl.pallas_call(
        kernel,
        out_shape=jax.ShapeDtypeStruct((ROWS, NZ * HALF), bf),
        in_specs=[pl.BlockSpec(memory_space=pltpu.VMEM)] * 6,
        out_specs=pl.BlockSpec(memory_space=pltpu.VMEM),
        scratch_shapes=[
            pltpu.VMEM((NZ, STRIP, WIDE), bf),
            pltpu.VMEM((NZ, 2, HALF, HEADS * NOPE), bf),
            pltpu.VMEM((WIDE, TOTAL), bf),
            pltpu.VMEM((HEADS * NOPE, LATENT), bf),
            pltpu.VMEM((1, TOTAL), jnp.float32),
            pltpu.VMEM((1, TOTAL), jnp.float32),
            pltpu.VMEM((LATENT, TOTAL), jnp.float32),
            pltpu.VMEM((HEADS * NOPE, STRIP), bf),
            pltpu.VMEM((NZ, 2, 4, HALF, ROWS), bf),
            pltpu.VMEM((NZ, HEADS, HALF, ROWS), bf),
            pltpu.VMEM((NZ, HALF, ROWS), bf),
            pltpu.VMEM((NZ * HALF, ROWS), bf),
            dma((NZ,)), dma((NZ,)),
            dma((NZ, 3)), dma((NZ, 3)),
            dma((NZ, 2)), dma((NZ, 2)),
            dma((NZ, 2)), dma((NZ, 2)),
            dma((7,)), dma((7,)),
            dma((7,)), dma((7,)),
            dma((2,)), dma((2,)),
            dma((2,)), dma((2,)),
            dma((2,)), dma((2,)),
            dma((NZ, 2, 4)), dma((NZ, HEADS)),
            dma((NZ,)), dma((NZ,)),
        ],
        compiler_params=pltpu.CompilerParams(
            collective_id=0, has_side_effects=True, vmem_limit_bytes=56 * 1024 * 1024),
        name="layer",
    )(queries, compressed, latent_gain.reshape(1, LATENT), w_uk, w_uv, w_out)


def solution(mesh):
    return jax.shard_map(
        on_device,
        mesh=mesh,
        in_specs=(
            P("ctx", "head"),
            P("ctx", None),
            P(),
            P(None, "head"),
            P(None, "head"),
            P("head", "ctx"),
        ),
        out_specs=P("ctx", "head"),
        check_vma=False,
    )
```

```python
import math

import jax
import jax.numpy as jnp
from jax import lax
from jax.experimental import pallas as pl
from jax.experimental.pallas import tpu as pltpu
from jax.sharding import PartitionSpec as P

LATENT = 512
ROPE = 64
NOPE = 128
HD = NOPE + ROPE
WIDE = 640
ROWS = 128
HEADS = 8
STRIP = 4 * ROWS
TOTAL = HEADS * ROWS
CHUNK = 512
HALF = 112
NZ = 8
SCALE = HD ** -0.5 * math.log2(math.e)
NT = (((1,), (1,)), ((), ()))
MESH = pl.DeviceIdType.MESH


def al(value, unit):
    return pl.multiple_of(value, unit)


def kernel(q_ref, comp_ref, gain_ref, uk_ref, uv_ref, w_ref, out_ref,
           lat, ball, qt, uvt, m_ref, l_ref, acc, abuf, cbuf, rbuf, fsrc, fin,
           s1s, s1r, s2s, s2r, s3s, s3r, s4s, s4r, sws, swr, brs, brr, bls, blr,
           axs, axr, ars, arr, acs, acr, cs, cr, fs, fr):
    ctx = lax.axis_index("ctx")
    head = lax.axis_index("head")
    z = ctx // 4
    j = ctx % 4
    y = head // 2
    xh = head % 2
    xl = j // 2
    base = 4 * z
    sib = j + 1 - 2 * (j % 2)
    opp = (j + 2) % 4
    opp_sib = (sib + 2) % 4
    up_xh = (xh + xl) % 2
    down_xh = 1 - up_xh
    over = (ctx, 2 * y + 1 - xh)
    core = (base + sib, head)
    x_up = (base + opp, 2 * y + up_xh)
    x_down = (base + opp, 2 * y + down_xh)
    z_up = (4 * ((z + 1) % NZ) + j, head)
    z_down = (4 * ((z + 7) % NZ) + j, head)

    def copy(src, dst, send, recv, device):
        return pltpu.make_async_remote_copy(
            src_ref=src, dst_ref=dst, send_sem=send, recv_sem=recv, device_id=device, device_id_type=MESH)

    def arrived(dst, recv):
        copy(dst, dst, recv, recv, core).wait_recv()

    def left(src, send):
        copy(src, src, send, send, core).wait_send()

    barrier = pltpu.get_barrier_semaphore()

    def greet(device):
        pl.semaphore_signal(barrier, inc=1, device_id=device, device_id_type=MESH)

    for k in range(1, NZ):
        greet((4 * ((z + k) % NZ) + j, head))
    for k in range(1, 4):
        greet((ctx, 2 * ((y + k) % 4) + xh))
    greet(over)
    greet(x_up)
    greet(x_down)
    greet(core)
    for p in range(4):
        for b in range(2):
            @pl.when((p != j) | (j != y) | (b != xh))
            def _():
                greet((base + p, 2 * j + b))

    comp = comp_ref[...].T
    own = comp[:, :LATENT].astype(jnp.float32)
    mean_square = jnp.mean(own * own, axis=1, keepdims=True)
    normed = (own * lax.rsqrt(mean_square + 1e-06) * gain_ref[...]).astype(jnp.bfloat16)
    mine = pl.ds(al(j * ROWS, ROWS), ROWS)
    lat[z, mine, :LATENT] = normed
    lat[z, mine, LATENT:] = jnp.concatenate(
        [comp[:, LATENT:], jnp.zeros((ROWS, WIDE - LATENT - ROPE), jnp.bfloat16)], axis=1)
    ball[z, xh] = w_ref[pl.ds(al(xh * HALF, 16), HALF), :]

    pl.semaphore_wait(barrier, jnp.where(j == y, 21, 22))

    def rows_of(zs, member, start, count):
        return lat.at[zs, pl.ds(al(member * ROWS + start, 16), count), :]

    def z_copy(k):
        part = rows_of(z, j, y * 32, 32)
        return copy(part, part, s1s.at[k], s1r.at[z], (4 * (z + k) + j, head))

    for k in range(1, NZ):
        @pl.when(z + k < NZ)
        def _():
            z_copy(k).start()

    def y_copy(zs, k):
        part = rows_of(zs, j, y * 32, 32)
        return copy(part, part, s2s.at[zs, k - 1], s2r.at[zs, k - 1], (ctx, 2 * ((y + k) % 4) + xh))

    def x_copies(zs):
        low = rows_of(zs, j, 0, 64)
        high = rows_of(zs, j, 64, 64)
        return (copy(low, low, s3s.at[zs, 0], s3r.at[zs, 0], x_up),
                copy(high, high, s3s.at[zs, 1], s3r.at[zs, 1], x_down))

    def core_copy(zs, member, slot):
        part = rows_of(zs, member, 0, ROWS)
        return copy(part, part, s4s.at[zs, slot], s4r.at[zs, slot], core)

    def stage1(d):
        zs = z - d
        arrived(rows_of(zs, j, y * 32, 32), s1r.at[zs])
        for k in range(1, 4):
            y_copy(zs, k).start()

    def stage2(d, wait=True):
        zs = z - d
        if wait:
            for k in range(1, 4):
                arrived(rows_of(zs, j, ((y + 4 - k) % 4) * 32, 32), s2r.at[zs, k - 1])
        for each in x_copies(zs):
            each.start()
        core_copy(zs, j, 0).start()

    def stage3(d):
        zs = z - d
        arrived(rows_of(zs, opp, 0, 64), s3r.at[zs, 0])
        arrived(rows_of(zs, opp, 64, 64), s3r.at[zs, 1])
        core_copy(zs, opp, 1).start()

    def stage4(d):
        zs = z - d
        arrived(rows_of(zs, sib, 0, ROWS), s4r.at[zs, 0])
        arrived(rows_of(zs, opp_sib, 0, ROWS), s4r.at[zs, 1])

    swap = copy(w_ref.at[pl.ds(al((1 - xh) * HALF, 16), HALF), :], ball.at[z, xh], sws, swr, over)

    def ring_up(u):
        part = ball.at[(z + NZ - u // 2) % NZ, (xh + u) % 2]
        return copy(part, part, brs.at[u], brr.at[u], z_up)

    def ring_down(u):
        part = ball.at[(z + u // 2) % NZ, (xh + u + u // 6) % 2]
        return copy(part, part, bls.at[u], blr.at[u], z_down)

    def ring_arrived(k):
        arrived(ball.at[(z + 7 - k // 2) % NZ, (xh + k) % 2], brr.at[k])
        arrived(ball.at[(z + 1 + k // 2) % NZ, (xh + k + k // 6) % 2], blr.at[k])

    def forward(k):
        ring_arrived(k)

        @pl.when(k < 5)
        def _():
            ring_up(k + 2).start()

        @pl.when(k < 4)
        def _():
            ring_down(k + 2).start()

        @pl.when(k == 5)
        def _():
            ring_down(6).start()

    def when_in(d, act):
        @pl.when(d <= z)
        def _():
            act(d)

    stage2(0, wait=False)
    swap.start()

    def absorb(h):
        lanes = slice(h * ROWS, (h + 1) * ROWS)
        qa = lax.dot_general(uk_ref[:, h * NOPE:(h + 1) * NOPE], q_ref[:, h * HD:h * HD + NOPE], NT,
                             preferred_element_type=jnp.float32)
        qt[:LATENT, lanes] = (qa * SCALE).astype(jnp.bfloat16)
        qr = q_ref[:, h * HD + NOPE:(h + 1) * HD].astype(jnp.float32) * SCALE
        qt[LATENT:LATENT + ROPE, lanes] = qr.T.astype(jnp.bfloat16)

    qt[LATENT + ROPE:, :] = jnp.zeros((WIDE - LATENT - ROPE, TOTAL), jnp.bfloat16)
    for h in range(HEADS):
        absorb(h)
    ring_up(0).start()
    ring_down(0).start()
    when_in(1, stage1)
    when_in(2, stage1)
    uvt[...] = uv_ref[...].T
    when_in(3, stage1)
    stage3(0)
    arrived(ball.at[z, 1 - xh], swr)
    ring_up(1).start()
    ring_down(1).start()
    when_in(1, stage2)
    when_in(4, stage1)
    when_in(2, stage2)
    when_in(5, stage1)
    when_in(3, stage2)

    def visit(zs, first):
        block = lat[zs]
        turned = block[:, :LATENT].T

        def score(c):
            s = jnp.dot(block, qt[:, c * CHUNK:(c + 1) * CHUNK], preferred_element_type=jnp.float32)
            if first:
                row = j * ROWS + lax.broadcasted_iota(jnp.int32, s.shape, 1) % ROWS
                s = jnp.where(row >= lax.broadcasted_iota(jnp.int32, s.shape, 0), s, -jnp.inf)
            return s

        def rest(s, c):
            lanes = slice(c * CHUNK, (c + 1) * CHUNK)
            m_new = jnp.max(s, axis=0, keepdims=True)
            if not first:
                m_old = m_ref[:, lanes]
                m_new = jnp.maximum(m_old, m_new)
                alpha = jnp.exp2(m_old - m_new)
            p = jnp.exp2(s - m_new)
            total = jnp.sum(p, axis=0, keepdims=True)
            part = jnp.dot(turned, p.astype(jnp.bfloat16), preferred_element_type=jnp.float32)
            m_ref[:, lanes] = m_new
            if first:
                l_ref[:, lanes] = total
                acc[:, lanes] = part
            else:
                l_ref[:, lanes] = l_ref[:, lanes] * alpha + total
                acc[:, lanes] = acc[:, lanes] * alpha + part

        s = score(0)
        later = score(1)
        rest(s, 0)
        rest(later, 1)

    def ahead(i):
        when_in(i + 6, stage1)
        when_in(i + 4, stage2)

    when_in(1, stage3)
    stage4(0)
    visit(z, True)
    ahead(0)
    forward(0)

    @pl.loop(1, z + 1)
    def _(i):
        when_in(i + 1, stage3)
        stage4(i)
        visit(z - i, False)
        ahead(i)

        @pl.when(i % 2 == 1)
        def _():
            forward((i + 1) // 2)

    done = jnp.maximum(2, 1 + (z + 1) // 2)

    def piece(across, member, c, start=0, count=CHUNK):
        return abuf.at[across, pl.ds(c * CHUNK + start, count), pl.ds(al(member * ROWS, ROWS), ROWS)]

    def a_sends(c):
        part = piece(xh, j, c)
        return (copy(part, part, axs.at[c, 0], axr.at[c, 0], x_up),
                copy(part, part, axs.at[c, 1], axr.at[c, 1], x_down),
                copy(part, part, acs.at[c, 0], acr.at[c, 0], core))

    def a_from_down(c):
        part, half = piece(down_xh, opp, c), piece(down_xh, opp, c, 0, CHUNK // 2)
        return (copy(half, half, ars.at[c, 0], arr.at[c, 0], x_up),
                copy(part, part, acs.at[c, 1], acr.at[c, 1], core))

    def a_from_up(c):
        part, half = piece(up_xh, opp, c), piece(up_xh, opp, c, CHUNK // 2, CHUNK // 2)
        return (copy(half, half, ars.at[c, 1], arr.at[c, 1], x_down),
                copy(part, part, acs.at[c, 2], acr.at[c, 2], core))

    def a_across(c):
        part = piece(1 - xh, j, c)
        return copy(part, part, acs.at[c, 3], acr.at[c, 3], core)

    for c in range(2):
        for h in range(c * 4, c * 4 + 4):
            lanes = slice(h * ROWS, (h + 1) * ROWS)
            o = (acc[:, lanes] / l_ref[:, lanes]).astype(jnp.bfloat16)
            a = jnp.dot(uvt[h * NOPE:(h + 1) * NOPE, :], o, preferred_element_type=jnp.float32)
            abuf[xh, h * NOPE:(h + 1) * NOPE, mine] = a.astype(jnp.bfloat16)
        for each in a_sends(c):
            each.start()
    for c in range(2):
        arrived(piece(down_xh, opp, c), axr.at[c, 0])
        for each in a_from_down(c):
            each.start()
        arrived(piece(up_xh, opp, c), axr.at[c, 1])
        for each in a_from_up(c):
            each.start()

    @pl.when(z == 0)
    def _():
        forward(1)

    for c in range(2):
        arrived(piece(1 - xh, j, c, 0, CHUNK // 2), arr.at[c, 0])
        arrived(piece(1 - xh, j, c, CHUNK // 2, CHUNK // 2), arr.at[c, 1])
        a_across(c).start()
    for c in range(2):
        arrived(piece(xh, sib, c), acr.at[c, 0])
        arrived(piece(down_xh, opp_sib, c), acr.at[c, 1])
        arrived(piece(up_xh, opp_sib, c), acr.at[c, 2])
        arrived(piece(1 - xh, sib, c), acr.at[c, 3])

    def home(s):
        far = (s + 1) // 2
        return (z + NZ + far * (1 - 2 * (s % 2))) % NZ

    def c_copy(s, t):
        return copy(cbuf.at[s, t], rbuf.at[s, y], cs.at[s, t], cr.at[s, y], (ctx, 2 * t + xh))

    def each_copy(s, act):
        for t in range(4):
            @pl.when(t != y)
            def _():
                act(c_copy(s, t))

    def multiply(slots):
        ct = None
        for across in range(2):
            blocks = [ball[home(s), across] for s in slots]
            rows = jnp.concatenate(blocks, axis=0) if len(blocks) > 1 else blocks[0]
            part = jnp.dot(rows, abuf[across], preferred_element_type=jnp.float32)
            ct = part if ct is None else ct + part
        ct = ct.astype(jnp.bfloat16)
        for r, s in enumerate(slots):
            for t in range(4):
                cbuf[s, t] = ct[r * HALF:(r + 1) * HALF, t * ROWS:(t + 1) * ROWS]
            each_copy(s, lambda each: each.start())

    spot = fin.at[pl.ds(al((2 * j + xh) * HALF, HALF), HALF), :]

    def f_copy(s):
        return copy(fsrc.at[s], spot, fs.at[s], fr.at[2 * j + xh], (base + y, home(s)))

    def is_here(s):
        return (y == j) & (home(s) == head)

    def gather(s):
        for k in range(1, 4):
            peer = (y + k) % 4
            arrived(rbuf.at[s, peer], cr.at[s, peer])
        total = cbuf[s, y].astype(jnp.float32)
        for k in range(1, 4):
            total = total + rbuf[s, (y + k) % 4].astype(jnp.float32)
        fsrc[s] = total.astype(jnp.bfloat16)
        here = is_here(s)

        @pl.when(here)
        def _():
            spot[...] = fsrc[s]

        @pl.when(jnp.logical_not(here))
        def _():
            f_copy(s).start()

    def reach(k):
        @pl.when(k >= done)
        def _():
            forward(k)

    multiply([0])

    @pl.loop(1, 4)
    def _(g):
        reach(2 * g - 2)
        reach(2 * g - 1)
        multiply([2 * g - 1, 2 * g])

        @pl.when(g == 1)
        def _():
            gather(0)

        @pl.when(g > 1)
        def _():
            gather(2 * g - 3)
            gather(2 * g - 2)

    reach(6)
    multiply([7])
    for s in range(5, 8):
        gather(s)

    for p in range(4):
        for b in range(2):
            @pl.when((p != j) | (j != y) | (b != xh))
            def _():
                arrived(fin.at[pl.ds((2 * p + b) * HALF, HALF), :], fr.at[2 * p + b])
    out_ref[...] = fin[...]

    for k in range(1, NZ):
        @pl.when(z + k < NZ)
        def _():
            z_copy(k).wait_send()

    @pl.loop(0, z + 1)
    def _(zs):
        @pl.when(zs < z)
        def _():
            for k in range(1, 4):
                y_copy(zs, k).wait_send()
        for each in x_copies(zs):
            each.wait_send()
        core_copy(zs, j, 0).wait_send()
        core_copy(zs, opp, 1).wait_send()

    swap.wait_send()

    @pl.loop(0, 7)
    def _(u):
        ring_up(u).wait_send()
        ring_down(u).wait_send()

    for c in range(2):
        for each in a_sends(c) + a_from_down(c) + a_from_up(c) + (a_across(c),):
            each.wait_send()

    @pl.loop(0, NZ)
    def _(s):
        each_copy(s, lambda each: each.wait_send())

        @pl.when(jnp.logical_not(is_here(s)))
        def _():
            f_copy(s).wait_send()


def on_device(queries, compressed, latent_gain, w_uk, w_uv, w_out):
    dma = pltpu.SemaphoreType.DMA
    bf = jnp.bfloat16
    return pl.pallas_call(
        kernel,
        out_shape=jax.ShapeDtypeStruct((NZ * HALF, ROWS), bf),
        in_specs=[pl.BlockSpec(memory_space=pltpu.VMEM)] * 6,
        out_specs=pl.BlockSpec(memory_space=pltpu.VMEM),
        scratch_shapes=[
            pltpu.VMEM((NZ, STRIP, WIDE), bf),
            pltpu.VMEM((NZ, 2, HALF, HEADS * NOPE), bf),
            pltpu.VMEM((WIDE, TOTAL), bf),
            pltpu.VMEM((HEADS * NOPE, LATENT), bf),
            pltpu.VMEM((1, TOTAL), jnp.float32),
            pltpu.VMEM((1, TOTAL), jnp.float32),
            pltpu.VMEM((LATENT, TOTAL), jnp.float32),
            pltpu.VMEM((2, HEADS * NOPE, STRIP), bf),
            pltpu.VMEM((NZ, 4, HALF, ROWS), bf),
            pltpu.VMEM((NZ, 4, HALF, ROWS), bf),
            pltpu.VMEM((NZ, HALF, ROWS), bf),
            pltpu.VMEM((NZ * HALF, ROWS), bf),
            dma((NZ,)), dma((NZ,)),
            dma((NZ, 3)), dma((NZ, 3)),
            dma((NZ, 2)), dma((NZ, 2)),
            dma((NZ, 2)), dma((NZ, 2)),
            dma, dma,
            dma((7,)), dma((7,)),
            dma((7,)), dma((7,)),
            dma((2, 2)), dma((2, 2)),
            dma((2, 2)), dma((2, 2)),
            dma((2, 4)), dma((2, 4)),
            dma((NZ, 4)), dma((NZ, 4)),
            dma((NZ,)), dma((NZ,)),
        ],
        compiler_params=pltpu.CompilerParams(
            collective_id=0, has_side_effects=True, vmem_limit_bytes=56 * 1024 * 1024),
        name="layer",
    )(queries, compressed.T, latent_gain.reshape(1, LATENT), w_uk, w_uv, w_out.T).T


def solution(mesh):
    return jax.shard_map(
        on_device,
        mesh=mesh,
        in_specs=(
            P("ctx", "head"),
            P("ctx", None),
            P(),
            P(None, "head"),
            P(None, "head"),
            P("head", "ctx"),
        ),
        out_specs=P("ctx", "head"),
        check_vma=False,
    )
```

```python
import math

import jax
import jax.numpy as jnp
from jax import lax
from jax.experimental import pallas as pl
from jax.experimental.pallas import tpu as pltpu
from jax.sharding import PartitionSpec as P

LATENT = 512
ROPE = 64
NOPE = 128
HD = NOPE + ROPE
WIDE = 640
ROWS = 128
HEADS = 8
STRIP = 4 * ROWS
TOTAL = HEADS * ROWS
CHUNK = 512
HALF = 112
NZ = 8
SCALE = HD ** -0.5 * math.log2(math.e)
NT = (((1,), (1,)), ((), ()))
MESH = pl.DeviceIdType.MESH


def al(value, unit):
    return pl.multiple_of(value, unit)


def kernel(q_hbm, comp_hbm, gain_ref, uk_hbm, uv_hbm, w_hbm, out_ref,
           q_ref, comp_ref, uk_ref, uv_ref, w_ref, loads,
           lat, ball, qt, uvt, m_ref, l_ref, acc, abuf, cbuf, rbuf, fsrc, fin,
           s1s, s1r, s2s, s2r, s3s, s3r, s4s, s4r, sws, swr, brs, brr, bls, blr,
           axs, axr, ars, arr, acs, acr, cs, cr, fs, fr):
    ctx = lax.axis_index("ctx")
    head = lax.axis_index("head")
    z = ctx // 4
    j = ctx % 4
    y = head // 2
    xh = head % 2
    xl = j // 2
    base = 4 * z
    sib = j + 1 - 2 * (j % 2)
    opp = (j + 2) % 4
    opp_sib = (sib + 2) % 4
    up_xh = (xh + xl) % 2
    down_xh = 1 - up_xh
    over = (ctx, 2 * y + 1 - xh)
    core = (base + sib, head)
    x_up = (base + opp, 2 * y + up_xh)
    x_down = (base + opp, 2 * y + down_xh)
    z_up = (4 * ((z + 1) % NZ) + j, head)
    z_down = (4 * ((z + 7) % NZ) + j, head)

    def copy(src, dst, send, recv, device):
        return pltpu.make_async_remote_copy(
            src_ref=src, dst_ref=dst, send_sem=send, recv_sem=recv, device_id=device, device_id_type=MESH)

    def arrived(dst, recv):
        copy(dst, dst, recv, recv, core).wait_recv()

    def left(src, send):
        copy(src, src, send, send, core).wait_send()

    fetch = [pltpu.make_async_copy(a, b, loads.at[n]) for n, (a, b) in enumerate((
        (comp_hbm, comp_ref), (w_hbm, w_ref), (q_hbm, q_ref), (uk_hbm, uk_ref), (uv_hbm, uv_ref)))]
    for each in fetch:
        each.start()

    barrier = pltpu.get_barrier_semaphore()

    def greet(device):
        pl.semaphore_signal(barrier, inc=1, device_id=device, device_id_type=MESH)

    for k in range(1, NZ):
        greet((4 * ((z + k) % NZ) + j, head))
    for k in range(1, 4):
        greet((ctx, 2 * ((y + k) % 4) + xh))
    greet(over)
    greet(x_up)
    greet(x_down)
    greet(core)
    for p in range(4):
        for b in range(2):
            @pl.when((p != j) | (j != y) | (b != xh))
            def _():
                greet((base + p, 2 * j + b))

    fetch[0].wait()
    comp = comp_ref[...].T
    own = comp[:, :LATENT].astype(jnp.float32)
    mean_square = jnp.mean(own * own, axis=1, keepdims=True)
    normed = (own * lax.rsqrt(mean_square + 1e-06) * gain_ref[...]).astype(jnp.bfloat16)
    mine = pl.ds(al(j * ROWS, ROWS), ROWS)
    lat[z, mine, :LATENT] = normed
    lat[z, mine, LATENT:] = jnp.concatenate(
        [comp[:, LATENT:], jnp.zeros((ROWS, WIDE - LATENT - ROPE), jnp.bfloat16)], axis=1)
    fetch[1].wait()
    ball[z, xh] = w_ref[pl.ds(al(xh * HALF, 16), HALF), :]

    pl.semaphore_wait(barrier, jnp.where(j == y, 21, 22))

    def rows_of(zs, member, start, count):
        return lat.at[zs, pl.ds(al(member * ROWS + start, 16), count), :]

    def z_copy(k):
        part = rows_of(z, j, y * 32, 32)
        return copy(part, part, s1s.at[k], s1r.at[z], (4 * (z + k) + j, head))

    for k in range(1, NZ):
        @pl.when(z + k < NZ)
        def _():
            z_copy(k).start()

    def y_copy(zs, k):
        part = rows_of(zs, j, y * 32, 32)
        return copy(part, part, s2s.at[zs, k - 1], s2r.at[zs, k - 1], (ctx, 2 * ((y + k) % 4) + xh))

    def x_copies(zs):
        low = rows_of(zs, j, 0, 64)
        high = rows_of(zs, j, 64, 64)
        return (copy(low, low, s3s.at[zs, 0], s3r.at[zs, 0], x_up),
                copy(high, high, s3s.at[zs, 1], s3r.at[zs, 1], x_down))

    def core_copy(zs, member, slot):
        part = rows_of(zs, member, 0, ROWS)
        return copy(part, part, s4s.at[zs, slot], s4r.at[zs, slot], core)

    def stage1(d):
        zs = z - d
        arrived(rows_of(zs, j, y * 32, 32), s1r.at[zs])
        for k in range(1, 4):
            y_copy(zs, k).start()

    def stage2(d, wait=True):
        zs = z - d
        if wait:
            for k in range(1, 4):
                arrived(rows_of(zs, j, ((y + 4 - k) % 4) * 32, 32), s2r.at[zs, k - 1])
        for each in x_copies(zs):
            each.start()
        core_copy(zs, j, 0).start()

    def stage3(d):
        zs = z - d
        arrived(rows_of(zs, opp, 0, 64), s3r.at[zs, 0])
        arrived(rows_of(zs, opp, 64, 64), s3r.at[zs, 1])
        core_copy(zs, opp, 1).start()

    def stage4(d):
        zs = z - d
        arrived(rows_of(zs, sib, 0, ROWS), s4r.at[zs, 0])
        arrived(rows_of(zs, opp_sib, 0, ROWS), s4r.at[zs, 1])

    swap = copy(w_ref.at[pl.ds(al((1 - xh) * HALF, 16), HALF), :], ball.at[z, xh], sws, swr, over)

    def ring_up(u):
        part = ball.at[(z + NZ - u // 2) % NZ, (xh + u) % 2]
        return copy(part, part, brs.at[u], brr.at[u], z_up)

    def ring_down(u):
        part = ball.at[(z + u // 2) % NZ, (xh + u + u // 6) % 2]
        return copy(part, part, bls.at[u], blr.at[u], z_down)

    def ring_arrived(k):
        arrived(ball.at[(z + 7 - k // 2) % NZ, (xh + k) % 2], brr.at[k])
        arrived(ball.at[(z + 1 + k // 2) % NZ, (xh + k + k // 6) % 2], blr.at[k])

    def forward(k):
        ring_arrived(k)

        @pl.when(k < 5)
        def _():
            ring_up(k + 2).start()

        @pl.when(k < 4)
        def _():
            ring_down(k + 2).start()

        @pl.when(k == 5)
        def _():
            ring_down(6).start()

    def when_in(d, act):
        @pl.when(d <= z)
        def _():
            act(d)

    swap.start()
    stage2(0, wait=False)
    ring_up(0).start()
    ring_down(0).start()

    def absorb(h):
        lanes = slice(h * ROWS, (h + 1) * ROWS)
        qa = lax.dot_general(uk_ref[:, h * NOPE:(h + 1) * NOPE], q_ref[:, h * HD:h * HD + NOPE], NT,
                             preferred_element_type=jnp.float32)
        qt[:LATENT, lanes] = (qa * SCALE).astype(jnp.bfloat16)
        qr = q_ref[:, h * HD + NOPE:(h + 1) * HD].astype(jnp.float32) * SCALE
        qt[LATENT:LATENT + ROPE, lanes] = qr.T.astype(jnp.bfloat16)

    qt[LATENT + ROPE:, :] = jnp.zeros((WIDE - LATENT - ROPE, TOTAL), jnp.bfloat16)
    fetch[2].wait()
    fetch[3].wait()
    for h in range(HEADS):
        absorb(h)
    fetch[4].wait()
    uvt[...] = uv_ref[...].T
    for d in range(1, 4):
        when_in(d, stage1)
    arrived(ball.at[z, 1 - xh], swr)
    ring_up(1).start()
    ring_down(1).start()
    when_in(1, stage2)
    when_in(4, stage1)
    when_in(5, stage1)
    forward(0)
    when_in(2, stage2)
    stage3(0)
    when_in(3, stage2)

    def visit(zs, first, chunk=None):
        block = lat[zs]
        turned = block[:, :LATENT].T

        def score(c):
            s = jnp.dot(block, qt[:, c * CHUNK:(c + 1) * CHUNK], preferred_element_type=jnp.float32)
            if first:
                row = j * ROWS + lax.broadcasted_iota(jnp.int32, s.shape, 1) % ROWS
                s = jnp.where(row >= lax.broadcasted_iota(jnp.int32, s.shape, 0), s, -jnp.inf)
            return s

        def rest(s, c):
            lanes = slice(c * CHUNK, (c + 1) * CHUNK)
            m_new = jnp.max(s, axis=0, keepdims=True)
            if not first:
                m_old = m_ref[:, lanes]
                m_new = jnp.maximum(m_old, m_new)
                alpha = jnp.exp2(m_old - m_new)
            p = jnp.exp2(s - m_new)
            total = jnp.sum(p, axis=0, keepdims=True)
            part = jnp.dot(turned, p.astype(jnp.bfloat16), preferred_element_type=jnp.float32)
            m_ref[:, lanes] = m_new
            if first:
                l_ref[:, lanes] = total
                acc[:, lanes] = part
            else:
                l_ref[:, lanes] = l_ref[:, lanes] * alpha + total
                acc[:, lanes] = acc[:, lanes] * alpha + part

        if chunk is None:
            s = score(0)
            later = score(1)
            rest(s, 0)
            rest(later, 1)
        else:
            rest(score(chunk), chunk)

    def ahead(i):
        when_in(i + 6, stage1)
        when_in(i + 4, stage2)

    stage4(0)
    visit(z, True)
    when_in(1, stage3)
    ahead(0)
    forward(1)

    @pl.loop(1, z)
    def _(i):
        when_in(i + 1, stage3)
        stage4(i)
        visit(z - i, False)
        ahead(i)

        @pl.when((i == 2) | (i == 4))
        def _():
            forward(1 + i // 2)

    def last_visit(c):
        @pl.when(z >= 1)
        def _():
            if c == 0:
                stage4(z)
            visit(0, False, c)

    done = jnp.minimum(1 + (z + 1) // 2, 4)

    def piece(across, member, c, start=0, count=CHUNK):
        return abuf.at[across, pl.ds(c * CHUNK + start, count), pl.ds(al(member * ROWS, ROWS), ROWS)]

    def a_sends(c):
        part = piece(xh, j, c)
        return (copy(part, part, axs.at[c, 0], axr.at[c, 0], x_up),
                copy(part, part, axs.at[c, 1], axr.at[c, 1], x_down),
                copy(part, part, acs.at[c, 0], acr.at[c, 0], core))

    def a_from_down(c):
        part, half = piece(down_xh, opp, c), piece(down_xh, opp, c, 0, CHUNK // 2)
        return (copy(half, half, ars.at[c, 0], arr.at[c, 0], x_up),
                copy(part, part, acs.at[c, 1], acr.at[c, 1], core))

    def a_from_up(c):
        part, half = piece(up_xh, opp, c), piece(up_xh, opp, c, CHUNK // 2, CHUNK // 2)
        return (copy(half, half, ars.at[c, 1], arr.at[c, 1], x_down),
                copy(part, part, acs.at[c, 2], acr.at[c, 2], core))

    def a_across(c):
        part = piece(1 - xh, j, c)
        return copy(part, part, acs.at[c, 3], acr.at[c, 3], core)

    for c in range(2):
        last_visit(c)
        for h in range(c * 4, c * 4 + 4):
            lanes = slice(h * ROWS, (h + 1) * ROWS)
            o = (acc[:, lanes] / l_ref[:, lanes]).astype(jnp.bfloat16)
            a = jnp.dot(uvt[h * NOPE:(h + 1) * NOPE, :], o, preferred_element_type=jnp.float32)
            abuf[xh, h * NOPE:(h + 1) * NOPE, mine] = a.astype(jnp.bfloat16)
        for each in a_sends(c):
            each.start()
        if c == 0:
            @pl.when(z >= 1)
            def _():
                forward(done)
    for c in range(2):
        arrived(piece(down_xh, opp, c), axr.at[c, 0])
        for each in a_from_down(c):
            each.start()
        arrived(piece(up_xh, opp, c), axr.at[c, 1])
        for each in a_from_up(c):
            each.start()

    @pl.when(z <= 4)
    def _():
        forward(done + 1)

    for c in range(2):
        arrived(piece(1 - xh, j, c, 0, CHUNK // 2), arr.at[c, 0])
        arrived(piece(1 - xh, j, c, CHUNK // 2, CHUNK // 2), arr.at[c, 1])
        a_across(c).start()
    forward(jnp.minimum(done + 2, 5))
    for c in range(2):
        arrived(piece(xh, sib, c), acr.at[c, 0])
        arrived(piece(down_xh, opp_sib, c), acr.at[c, 1])
        arrived(piece(up_xh, opp_sib, c), acr.at[c, 2])
        arrived(piece(1 - xh, sib, c), acr.at[c, 3])

    def home(s):
        far = (s + 1) // 2
        return (z + NZ + far * (1 - 2 * (s % 2))) % NZ

    def c_copy(s, t):
        return copy(cbuf.at[s, t], rbuf.at[s, y], cs.at[s, t], cr.at[s, y], (ctx, 2 * t + xh))

    def each_copy(s, act):
        for t in range(4):
            @pl.when(t != y)
            def _():
                act(c_copy(s, t))

    def multiply(slots):
        ct = None
        for across in range(2):
            blocks = [ball[home(s), across] for s in slots]
            rows = jnp.concatenate(blocks, axis=0) if len(blocks) > 1 else blocks[0]
            part = jnp.dot(rows, abuf[across], preferred_element_type=jnp.float32)
            ct = part if ct is None else ct + part
        ct = ct.astype(jnp.bfloat16)
        for r, s in enumerate(slots):
            for t in range(4):
                cbuf[s, t] = ct[r * HALF:(r + 1) * HALF, t * ROWS:(t + 1) * ROWS]
            each_copy(s, lambda each: each.start())

    spot = fin.at[pl.ds(al((2 * j + xh) * HALF, HALF), HALF), :]

    def f_copy(s):
        return copy(fsrc.at[s], spot, fs.at[s], fr.at[2 * j + xh], (base + y, home(s)))

    def is_here(s):
        return (y == j) & (home(s) == head)

    def gather(s):
        for k in range(1, 4):
            peer = (y + k) % 4
            arrived(rbuf.at[s, peer], cr.at[s, peer])
        total = cbuf[s, y].astype(jnp.float32)
        for k in range(1, 4):
            total = total + rbuf[s, (y + k) % 4].astype(jnp.float32)
        fsrc[s] = total.astype(jnp.bfloat16)
        here = is_here(s)

        @pl.when(here)
        def _():
            spot[...] = fsrc[s]

        @pl.when(jnp.logical_not(here))
        def _():
            f_copy(s).start()

    def reach(k):
        @pl.when(k >= jnp.minimum(done + 3, 6))
        def _():
            forward(k)

    multiply([0])

    @pl.loop(1, 4)
    def _(g):
        reach(2 * g - 2)
        reach(2 * g - 1)
        multiply([2 * g - 1, 2 * g])

        @pl.when(g == 1)
        def _():
            gather(0)

        @pl.when(g > 1)
        def _():
            gather(2 * g - 3)
            gather(2 * g - 2)

    reach(6)
    multiply([7])
    for s in range(5, 8):
        gather(s)

    for p in range(4):
        for b in range(2):
            @pl.when((p != j) | (j != y) | (b != xh))
            def _():
                arrived(fin.at[pl.ds((2 * p + b) * HALF, HALF), :], fr.at[2 * p + b])
    out_ref[...] = fin[...]

    for k in range(1, NZ):
        @pl.when(z + k < NZ)
        def _():
            z_copy(k).wait_send()

    @pl.loop(0, z + 1)
    def _(zs):
        @pl.when(zs < z)
        def _():
            for k in range(1, 4):
                y_copy(zs, k).wait_send()
        for each in x_copies(zs):
            each.wait_send()
        core_copy(zs, j, 0).wait_send()
        core_copy(zs, opp, 1).wait_send()

    swap.wait_send()

    @pl.loop(0, 7)
    def _(u):
        ring_up(u).wait_send()
        ring_down(u).wait_send()

    for c in range(2):
        for each in a_sends(c) + a_from_down(c) + a_from_up(c) + (a_across(c),):
            each.wait_send()

    @pl.loop(0, NZ)
    def _(s):
        each_copy(s, lambda each: each.wait_send())

        @pl.when(jnp.logical_not(is_here(s)))
        def _():
            f_copy(s).wait_send()


def on_device(queries, compressed, latent_gain, w_uk, w_uv, w_out):
    dma = pltpu.SemaphoreType.DMA
    bf = jnp.bfloat16
    return pl.pallas_call(
        kernel,
        out_shape=jax.ShapeDtypeStruct((NZ * HALF, ROWS), bf),
        in_specs=[pl.BlockSpec(memory_space=pltpu.VMEM if n == 2 else pl.ANY) for n in range(6)],
        out_specs=pl.BlockSpec(memory_space=pltpu.VMEM),
        scratch_shapes=[
            pltpu.VMEM((ROWS, HEADS * HD), bf),
            pltpu.VMEM((LATENT + ROPE, ROWS), bf),
            pltpu.VMEM((LATENT, HEADS * NOPE), bf),
            pltpu.VMEM((LATENT, HEADS * NOPE), bf),
            pltpu.VMEM((2 * HALF, HEADS * NOPE), bf),
            dma((5,)),
            pltpu.VMEM((NZ, STRIP, WIDE), bf),
            pltpu.VMEM((NZ, 2, HALF, HEADS * NOPE), bf),
            pltpu.VMEM((WIDE, TOTAL), bf),
            pltpu.VMEM((HEADS * NOPE, LATENT), bf),
            pltpu.VMEM((1, TOTAL), jnp.float32),
            pltpu.VMEM((1, TOTAL), jnp.float32),
            pltpu.VMEM((LATENT, TOTAL), jnp.float32),
            pltpu.VMEM((2, HEADS * NOPE, STRIP), bf),
            pltpu.VMEM((NZ, 4, HALF, ROWS), bf),
            pltpu.VMEM((NZ, 4, HALF, ROWS), bf),
            pltpu.VMEM((NZ, HALF, ROWS), bf),
            pltpu.VMEM((NZ * HALF, ROWS), bf),
            dma((NZ,)), dma((NZ,)),
            dma((NZ, 3)), dma((NZ, 3)),
            dma((NZ, 2)), dma((NZ, 2)),
            dma((NZ, 2)), dma((NZ, 2)),
            dma, dma,
            dma((7,)), dma((7,)),
            dma((7,)), dma((7,)),
            dma((2, 2)), dma((2, 2)),
            dma((2, 2)), dma((2, 2)),
            dma((2, 4)), dma((2, 4)),
            dma((NZ, 4)), dma((NZ, 4)),
            dma((NZ,)), dma((NZ,)),
        ],
        compiler_params=pltpu.CompilerParams(
            collective_id=0, has_side_effects=True, vmem_limit_bytes=56 * 1024 * 1024),
        name="layer",
    )(queries, compressed.T, latent_gain.reshape(1, LATENT), w_uk, w_uv, w_out.T).T


def solution(mesh):
    return jax.shard_map(
        on_device,
        mesh=mesh,
        in_specs=(
            P("ctx", "head"),
            P("ctx", None),
            P(),
            P(None, "head"),
            P(None, "head"),
            P("head", "ctx"),
        ),
        out_specs=P("ctx", "head"),
        check_vma=False,
    )
```

```python
import math

import jax
import jax.numpy as jnp
from jax import lax
from jax.experimental import pallas as pl
from jax.experimental.pallas import tpu as pltpu
from jax.sharding import PartitionSpec as P

LATENT = 512
ROPE = 64
NOPE = 128
HD = NOPE + ROPE
WIDE = 640
ROWS = 128
HEADS = 8
STRIP = 4 * ROWS
TOTAL = HEADS * ROWS
CHUNK = 512
PART = 256
HALF = 112
NZ = 8
SCALE = HD ** -0.5 * math.log2(math.e)
NT = (((1,), (1,)), ((), ()))
MESH = pl.DeviceIdType.MESH


def al(value, unit):
    return pl.multiple_of(value, unit)


def kernel(q_hbm, comp_hbm, gain_ref, uk_hbm, uv_hbm, w_hbm, out_ref,
           q_ref, comp_ref, uk_ref, uv_ref, w_ref, loads,
           lat, ball, qt, uvt, m_ref, l_ref, acc, abuf, cbuf, rbuf, fsrc, fin,
           s1s, s1r, s2s, s2r, s3s, s3r, s4s, s4r, sws, swr, brs, brr, bls, blr,
           axs, axr, ars, arr, acs, acr, cs, cr, fs, fr):
    ctx = lax.axis_index("ctx")
    head = lax.axis_index("head")
    z = ctx // 4
    j = ctx % 4
    y = head // 2
    xh = head % 2
    xl = j // 2
    base = 4 * z
    sib = j + 1 - 2 * (j % 2)
    opp = (j + 2) % 4
    opp_sib = (sib + 2) % 4
    up_xh = (xh + xl) % 2
    down_xh = 1 - up_xh
    over = (ctx, 2 * y + 1 - xh)
    core = (base + sib, head)
    x_up = (base + opp, 2 * y + up_xh)
    x_down = (base + opp, 2 * y + down_xh)
    z_up = (4 * ((z + 1) % NZ) + j, head)
    z_down = (4 * ((z + 7) % NZ) + j, head)

    def copy(src, dst, send, recv, device):
        return pltpu.make_async_remote_copy(
            src_ref=src, dst_ref=dst, send_sem=send, recv_sem=recv, device_id=device, device_id_type=MESH)

    def arrived(dst, recv):
        copy(dst, dst, recv, recv, core).wait_recv()

    def left(src, send):
        copy(src, src, send, send, core).wait_send()

    fetch = [pltpu.make_async_copy(a, b, loads.at[n]) for n, (a, b) in enumerate((
        (comp_hbm, comp_ref), (w_hbm, w_ref), (q_hbm, q_ref), (uk_hbm, uk_ref), (uv_hbm, uv_ref)))]
    for each in fetch:
        each.start()

    barrier = pltpu.get_barrier_semaphore()

    def greet(device):
        pl.semaphore_signal(barrier, inc=1, device_id=device, device_id_type=MESH)

    for k in range(1, NZ):
        greet((4 * ((z + k) % NZ) + j, head))
    for k in range(1, 4):
        greet((ctx, 2 * ((y + k) % 4) + xh))
    greet(over)
    greet(x_up)
    greet(x_down)
    greet(core)
    for p in range(4):
        for b in range(2):
            @pl.when((p != j) | (j != y) | (b != xh))
            def _():
                greet((base + p, 2 * j + b))

    fetch[0].wait()
    comp = comp_ref[...].T
    own = comp[:, :LATENT].astype(jnp.float32)
    mean_square = jnp.mean(own * own, axis=1, keepdims=True)
    normed = (own * lax.rsqrt(mean_square + 1e-06) * gain_ref[...]).astype(jnp.bfloat16)
    mine = pl.ds(al(j * ROWS, ROWS), ROWS)
    lat[z, mine, :LATENT] = normed
    lat[z, mine, LATENT:] = jnp.concatenate(
        [comp[:, LATENT:], jnp.zeros((ROWS, WIDE - LATENT - ROPE), jnp.bfloat16)], axis=1)
    fetch[1].wait()
    ball[z, xh] = w_ref[pl.ds(al(xh * HALF, 16), HALF), :]

    pl.semaphore_wait(barrier, jnp.where(j == y, 21, 22))

    def rows_of(zs, member, start, count):
        return lat.at[zs, pl.ds(al(member * ROWS + start, 16), count), :]

    def z_copy(k):
        part = rows_of(z, j, y * 32, 32)
        return copy(part, part, s1s.at[k], s1r.at[z], (4 * (z + k) + j, head))

    for k in range(1, NZ):
        @pl.when(z + k < NZ)
        def _():
            z_copy(k).start()

    def y_copy(zs, k):
        part = rows_of(zs, j, y * 32, 32)
        return copy(part, part, s2s.at[zs, k - 1], s2r.at[zs, k - 1], (ctx, 2 * ((y + k) % 4) + xh))

    def x_copies(zs):
        low = rows_of(zs, j, 0, 64)
        high = rows_of(zs, j, 64, 64)
        return (copy(low, low, s3s.at[zs, 0], s3r.at[zs, 0], x_up),
                copy(high, high, s3s.at[zs, 1], s3r.at[zs, 1], x_down))

    def core_copy(zs, member, slot):
        part = rows_of(zs, member, 0, ROWS)
        return copy(part, part, s4s.at[zs, slot], s4r.at[zs, slot], core)

    def stage1(d):
        zs = z - d
        arrived(rows_of(zs, j, y * 32, 32), s1r.at[zs])
        for k in range(1, 4):
            y_copy(zs, k).start()

    def stage2(d, wait=True):
        zs = z - d
        if wait:
            for k in range(1, 4):
                arrived(rows_of(zs, j, ((y + 4 - k) % 4) * 32, 32), s2r.at[zs, k - 1])
        for each in x_copies(zs):
            each.start()
        core_copy(zs, j, 0).start()

    def stage3(d):
        zs = z - d
        arrived(rows_of(zs, opp, 0, 64), s3r.at[zs, 0])
        arrived(rows_of(zs, opp, 64, 64), s3r.at[zs, 1])
        core_copy(zs, opp, 1).start()

    def stage4(d):
        zs = z - d
        arrived(rows_of(zs, sib, 0, ROWS), s4r.at[zs, 0])
        arrived(rows_of(zs, opp_sib, 0, ROWS), s4r.at[zs, 1])

    swap = copy(w_ref.at[pl.ds(al((1 - xh) * HALF, 16), HALF), :], ball.at[z, xh], sws, swr, over)

    def ring_up(u):
        part = ball.at[(z + NZ - u // 2) % NZ, (xh + u) % 2]
        return copy(part, part, brs.at[u], brr.at[u], z_up)

    def ring_down(u):
        part = ball.at[(z + u // 2) % NZ, (xh + u + u // 6) % 2]
        return copy(part, part, bls.at[u], blr.at[u], z_down)

    def ring_arrived(k):
        arrived(ball.at[(z + 7 - k // 2) % NZ, (xh + k) % 2], brr.at[k])
        arrived(ball.at[(z + 1 + k // 2) % NZ, (xh + k + k // 6) % 2], blr.at[k])

    def forward(k):
        ring_arrived(k)

        @pl.when(k < 5)
        def _():
            ring_up(k + 2).start()

        @pl.when(k < 4)
        def _():
            ring_down(k + 2).start()

        @pl.when(k == 5)
        def _():
            ring_down(6).start()

    def when_in(d, act):
        @pl.when(d <= z)
        def _():
            act(d)

    swap.start()
    stage2(0, wait=False)

    def absorb(h):
        lanes = slice(h * ROWS, (h + 1) * ROWS)
        qa = lax.dot_general(uk_ref[:, h * NOPE:(h + 1) * NOPE], q_ref[:, h * HD:h * HD + NOPE], NT,
                             preferred_element_type=jnp.float32)
        qt[:LATENT, lanes] = (qa * SCALE).astype(jnp.bfloat16)
        qr = q_ref[:, h * HD + NOPE:(h + 1) * HD].astype(jnp.float32) * SCALE
        qt[LATENT:LATENT + ROPE, lanes] = qr.T.astype(jnp.bfloat16)

    qt[LATENT + ROPE:, :] = jnp.zeros((WIDE - LATENT - ROPE, TOTAL), jnp.bfloat16)
    fetch[2].wait()
    fetch[3].wait()
    for h in range(HEADS):
        absorb(h)
    fetch[4].wait()
    uvt[...] = uv_ref[...].T
    for d in range(1, 4):
        when_in(d, stage1)
    for k in range(1, NZ):
        @pl.when(z + k < NZ)
        def _():
            z_copy(k).wait_send()
    ring_up(0).start()
    ring_down(0).start()
    arrived(ball.at[z, 1 - xh], swr)
    ring_up(1).start()
    ring_down(1).start()
    when_in(1, stage2)
    when_in(4, stage1)
    when_in(5, stage1)
    when_in(2, stage2)
    stage3(0)
    when_in(3, stage2)
    forward(0)

    def visit(zs, first, chunk=None):
        block = lat[zs]
        turned = block[:, :LATENT].T

        def score(c):
            s = jnp.dot(block, qt[:, c * CHUNK:(c + 1) * CHUNK], preferred_element_type=jnp.float32)
            if first:
                row = j * ROWS + lax.broadcasted_iota(jnp.int32, s.shape, 1) % ROWS
                s = jnp.where(row >= lax.broadcasted_iota(jnp.int32, s.shape, 0), s, -jnp.inf)
            return s

        def rest(s, c):
            lanes = slice(c * CHUNK, (c + 1) * CHUNK)
            m_new = jnp.max(s, axis=0, keepdims=True)
            if not first:
                m_old = m_ref[:, lanes]
                m_new = jnp.maximum(m_old, m_new)
                alpha = jnp.exp2(m_old - m_new)
            p = jnp.exp2(s - m_new)
            total = jnp.sum(p, axis=0, keepdims=True)
            part = jnp.dot(turned, p.astype(jnp.bfloat16), preferred_element_type=jnp.float32)
            m_ref[:, lanes] = m_new
            if first:
                l_ref[:, lanes] = total
                acc[:, lanes] = part
            else:
                l_ref[:, lanes] = l_ref[:, lanes] * alpha + total
                acc[:, lanes] = acc[:, lanes] * alpha + part

        if chunk is None:
            s = score(0)
            later = score(1)
            rest(s, 0)
            rest(later, 1)
        else:
            rest(score(chunk), chunk)

    def ahead(i):
        when_in(i + 6, stage1)
        when_in(i + 4, stage2)

    stage4(0)
    visit(z, True)
    when_in(1, stage3)
    ahead(0)

    @pl.loop(1, z)
    def _(i):
        when_in(i + 1, stage3)
        stage4(i)
        visit(z - i, False)
        ahead(i)

        @pl.when(jnp.where(z >= 5, (i == 2) | (i == 4), i % 2 == 1))
        def _():
            forward((i + 1) // 2)

    def last_visit(c):
        @pl.when(z >= 1)
        def _():
            if c == 0:
                stage4(z)
            visit(0, False, c)

    done = 1 + jnp.minimum(z, 4) // 2

    def piece(across, member, c, start=0, count=PART):
        return abuf.at[across, pl.ds(c * PART + start, count), pl.ds(al(member * ROWS, ROWS), ROWS)]

    def a_sends(c):
        part = piece(xh, j, c)
        return (copy(part, part, axs.at[c, 0], axr.at[c, 0], x_up),
                copy(part, part, axs.at[c, 1], axr.at[c, 1], x_down),
                copy(part, part, acs.at[c, 0], acr.at[c, 0], core))

    def a_from_down(c):
        part, half = piece(down_xh, opp, c), piece(down_xh, opp, c, 0, PART // 2)
        return (copy(half, half, ars.at[c, 0], arr.at[c, 0], x_up),
                copy(part, part, acs.at[c, 1], acr.at[c, 1], core))

    def a_from_up(c):
        part, half = piece(up_xh, opp, c), piece(up_xh, opp, c, PART // 2, PART // 2)
        return (copy(half, half, ars.at[c, 1], arr.at[c, 1], x_down),
                copy(part, part, acs.at[c, 2], acr.at[c, 2], core))

    def a_across(c):
        part = piece(1 - xh, j, c)
        return copy(part, part, acs.at[c, 3], acr.at[c, 3], core)

    for c in range(4):
        if c % 2 == 0:
            last_visit(c // 2)
        for h in range(c * 2, c * 2 + 2):
            lanes = slice(h * ROWS, (h + 1) * ROWS)
            o = (acc[:, lanes] / l_ref[:, lanes]).astype(jnp.bfloat16)
            a = jnp.dot(uvt[h * NOPE:(h + 1) * NOPE, :], o, preferred_element_type=jnp.float32)
            abuf[xh, h * NOPE:(h + 1) * NOPE, mine] = a.astype(jnp.bfloat16)
        for each in a_sends(c):
            each.start()
        if c == 1:
            forward(done)
    for c in range(4):
        arrived(piece(down_xh, opp, c), axr.at[c, 0])
        for each in a_from_down(c):
            each.start()
        arrived(piece(up_xh, opp, c), axr.at[c, 1])
        for each in a_from_up(c):
            each.start()

    forward(done + 1)

    for c in range(4):
        arrived(piece(1 - xh, j, c, 0, PART // 2), arr.at[c, 0])
        arrived(piece(1 - xh, j, c, PART // 2, PART // 2), arr.at[c, 1])
        a_across(c).start()
    forward(done + 2)
    for c in range(4):
        arrived(piece(xh, sib, c), acr.at[c, 0])
        arrived(piece(down_xh, opp_sib, c), acr.at[c, 1])
        arrived(piece(up_xh, opp_sib, c), acr.at[c, 2])
        arrived(piece(1 - xh, sib, c), acr.at[c, 3])

    def home(s):
        far = (s + 1) // 2
        return (z + NZ + far * (1 - 2 * (s % 2))) % NZ

    def c_copy(s, t):
        return copy(cbuf.at[s, t], rbuf.at[s, y], cs.at[s, t], cr.at[s, y], (ctx, 2 * t + xh))

    def each_copy(s, act):
        for t in range(4):
            @pl.when(t != y)
            def _():
                act(c_copy(s, t))

    def multiply(slots):
        ct = None
        for across in range(2):
            blocks = [ball[home(s), across] for s in slots]
            rows = jnp.concatenate(blocks, axis=0) if len(blocks) > 1 else blocks[0]
            part = jnp.dot(rows, abuf[across], preferred_element_type=jnp.float32)
            ct = part if ct is None else ct + part
        ct = ct.astype(jnp.bfloat16)
        for r, s in enumerate(slots):
            for t in range(4):
                cbuf[s, t] = ct[r * HALF:(r + 1) * HALF, t * ROWS:(t + 1) * ROWS]
            each_copy(s, lambda each: each.start())

    spot = fin.at[pl.ds(al((2 * j + xh) * HALF, HALF), HALF), :]

    def f_copy(s):
        return copy(fsrc.at[s], spot, fs.at[s], fr.at[2 * j + xh], (base + y, home(s)))

    def is_here(s):
        return (y == j) & (home(s) == head)

    def gather(s):
        for k in range(1, 4):
            peer = (y + k) % 4
            arrived(rbuf.at[s, peer], cr.at[s, peer])
        total = cbuf[s, y].astype(jnp.float32)
        for k in range(1, 4):
            total = total + rbuf[s, (y + k) % 4].astype(jnp.float32)
        fsrc[s] = total.astype(jnp.bfloat16)
        here = is_here(s)

        @pl.when(here)
        def _():
            spot[...] = fsrc[s]

        @pl.when(jnp.logical_not(here))
        def _():
            f_copy(s).start()

    def reach(k):
        @pl.when(k >= done + 3)
        def _():
            forward(k)

    multiply([0])

    @pl.loop(1, 4)
    def _(g):
        reach(2 * g - 2)
        reach(2 * g - 1)
        multiply([2 * g - 1, 2 * g])

        @pl.when(g == 2)
        def _():
            gather(0)

        @pl.when(g == 3)
        def _():
            gather(1)
            gather(2)

    reach(6)
    multiply([7])

    @pl.loop(3, NZ)
    def _(s):
        gather(s)

    for p in range(4):
        for b in range(2):
            @pl.when((p != j) | (j != y) | (b != xh))
            def _():
                arrived(fin.at[pl.ds((2 * p + b) * HALF, HALF), :], fr.at[2 * p + b])
    out_ref[...] = fin[...]

    @pl.loop(0, z + 1)
    def _(zs):
        @pl.when(zs < z)
        def _():
            for k in range(1, 4):
                y_copy(zs, k).wait_send()
        for each in x_copies(zs):
            each.wait_send()
        core_copy(zs, j, 0).wait_send()
        core_copy(zs, opp, 1).wait_send()

    swap.wait_send()

    @pl.loop(0, 7)
    def _(u):
        ring_up(u).wait_send()
        ring_down(u).wait_send()

    for c in range(4):
        for each in a_sends(c) + a_from_down(c) + a_from_up(c) + (a_across(c),):
            each.wait_send()

    @pl.loop(0, NZ)
    def _(s):
        each_copy(s, lambda each: each.wait_send())

        @pl.when(jnp.logical_not(is_here(s)))
        def _():
            f_copy(s).wait_send()


def on_device(queries, compressed, latent_gain, w_uk, w_uv, w_out):
    dma = pltpu.SemaphoreType.DMA
    bf = jnp.bfloat16
    return pl.pallas_call(
        kernel,
        out_shape=jax.ShapeDtypeStruct((NZ * HALF, ROWS), bf),
        in_specs=[pl.BlockSpec(memory_space=pltpu.VMEM if n == 2 else pl.ANY) for n in range(6)],
        out_specs=pl.BlockSpec(memory_space=pltpu.VMEM),
        scratch_shapes=[
            pltpu.VMEM((ROWS, HEADS * HD), bf),
            pltpu.VMEM((LATENT + ROPE, ROWS), bf),
            pltpu.VMEM((LATENT, HEADS * NOPE), bf),
            pltpu.VMEM((LATENT, HEADS * NOPE), bf),
            pltpu.VMEM((2 * HALF, HEADS * NOPE), bf),
            dma((5,)),
            pltpu.VMEM((NZ, STRIP, WIDE), bf),
            pltpu.VMEM((NZ, 2, HALF, HEADS * NOPE), bf),
            pltpu.VMEM((WIDE, TOTAL), bf),
            pltpu.VMEM((HEADS * NOPE, LATENT), bf),
            pltpu.VMEM((1, TOTAL), jnp.float32),
            pltpu.VMEM((1, TOTAL), jnp.float32),
            pltpu.VMEM((LATENT, TOTAL), jnp.float32),
            pltpu.VMEM((2, HEADS * NOPE, STRIP), bf),
            pltpu.VMEM((NZ, 4, HALF, ROWS), bf),
            pltpu.VMEM((NZ, 4, HALF, ROWS), bf),
            pltpu.VMEM((NZ, HALF, ROWS), bf),
            pltpu.VMEM((NZ * HALF, ROWS), bf),
            dma((NZ,)), dma((NZ,)),
            dma((NZ, 3)), dma((NZ, 3)),
            dma((NZ, 2)), dma((NZ, 2)),
            dma((NZ, 2)), dma((NZ, 2)),
            dma, dma,
            dma((7,)), dma((7,)),
            dma((7,)), dma((7,)),
            dma((4, 2)), dma((4, 2)),
            dma((4, 2)), dma((4, 2)),
            dma((4, 4)), dma((4, 4)),
            dma((NZ, 4)), dma((NZ, 4)),
            dma((NZ,)), dma((NZ,)),
        ],
        compiler_params=pltpu.CompilerParams(
            collective_id=0, has_side_effects=True, vmem_limit_bytes=56 * 1024 * 1024),
        name="layer",
    )(queries, compressed.T, latent_gain.reshape(1, LATENT), w_uk, w_uv, w_out.T).T


def solution(mesh):
    return jax.shard_map(
        on_device,
        mesh=mesh,
        in_specs=(
            P("ctx", "head"),
            P("ctx", None),
            P(),
            P(None, "head"),
            P(None, "head"),
            P("head", "ctx"),
        ),
        out_specs=P("ctx", "head"),
        check_vma=False,
    )
```

```python
import math

import jax
import jax.numpy as jnp
from jax import lax
from jax.experimental import pallas as pl
from jax.experimental.pallas import tpu as pltpu
from jax.sharding import PartitionSpec as P

LATENT = 512
ROPE = 64
NOPE = 128
HD = NOPE + ROPE
WIDE = 640
ROWS = 128
HEADS = 8
STRIP = 4 * ROWS
TOTAL = HEADS * ROWS
CHUNK = 512
PART = 256
HALF = 112
NZ = 8
SCALE = HD ** -0.5 * math.log2(math.e)
NT = (((1,), (1,)), ((), ()))
MESH = pl.DeviceIdType.MESH


def al(value, unit):
    return pl.multiple_of(value, unit)


def kernel(q_hbm, comp_hbm, gain_ref, uk_hbm, uv_hbm, w_hbm, out_ref,
           q_ref, comp_ref, uk_ref, uv_ref, w_ref, loads,
           lat, ball, qt, uvt, m_ref, l_ref, acc, abuf, cbuf, rbuf, fsrc, fin,
           s1s, s1r, s2s, s2r, s3s, s3r, s4s, s4r, sws, swr, brs, brr, bls, blr,
           axs, axr, ars, arr, acr, cs, cr, fs, fr):
    ctx = lax.axis_index("ctx")
    head = lax.axis_index("head")
    z = ctx // 4
    j = ctx % 4
    y = head // 2
    xh = head % 2
    xl = j // 2
    base = 4 * z
    sib = j + 1 - 2 * (j % 2)
    opp = (j + 2) % 4
    opp_sib = (sib + 2) % 4
    up_xh = (xh + xl) % 2
    down_xh = 1 - up_xh
    over = (ctx, 2 * y + 1 - xh)
    core = (base + sib, head)
    x_up = (base + opp, 2 * y + up_xh)
    x_down = (base + opp, 2 * y + down_xh)
    z_up = (4 * ((z + 1) % NZ) + j, head)
    z_down = (4 * ((z + 7) % NZ) + j, head)

    def copy(src, dst, send, recv, device):
        return pltpu.make_async_remote_copy(
            src_ref=src, dst_ref=dst, send_sem=send, recv_sem=recv, device_id=device, device_id_type=MESH)

    def arrived(dst, recv):
        copy(dst, dst, recv, recv, core).wait_recv()

    def left(src, send):
        copy(src, src, send, send, core).wait_send()

    fetch = [pltpu.make_async_copy(a, b, loads.at[n]) for n, (a, b) in enumerate((
        (comp_hbm, comp_ref), (w_hbm, w_ref), (q_hbm, q_ref), (uk_hbm, uk_ref), (uv_hbm, uv_ref)))]
    for each in fetch:
        each.start()

    barrier = pltpu.get_barrier_semaphore()

    def greet(device):
        pl.semaphore_signal(barrier, inc=1, device_id=device, device_id_type=MESH)

    for k in range(1, NZ):
        greet((4 * ((z + k) % NZ) + j, head))
    for k in range(1, 4):
        greet((ctx, 2 * ((y + k) % 4) + xh))
    greet(over)
    greet(x_up)
    greet(x_down)
    greet(core)
    for p in range(4):
        for b in range(2):
            @pl.when((p != j) | (j != y) | (b != xh))
            def _():
                greet((base + p, 2 * j + b))

    fetch[0].wait()
    comp = comp_ref[...].T
    own = comp[:, :LATENT].astype(jnp.float32)
    mean_square = jnp.mean(own * own, axis=1, keepdims=True)
    normed = (own * lax.rsqrt(mean_square + 1e-06) * gain_ref[...]).astype(jnp.bfloat16)
    mine = pl.ds(al(j * ROWS, ROWS), ROWS)
    lat[z, mine, :LATENT] = normed
    lat[z, mine, LATENT:] = jnp.concatenate(
        [comp[:, LATENT:], jnp.zeros((ROWS, WIDE - LATENT - ROPE), jnp.bfloat16)], axis=1)
    fetch[1].wait()
    ball[z, xh] = w_ref[pl.ds(al(xh * HALF, 16), HALF), :]

    pl.semaphore_wait(barrier, jnp.where(j == y, 21, 22))

    def rows_of(zs, member, start, count):
        return lat.at[zs, pl.ds(al(member * ROWS + start, 16), count), :]

    def z_copy(k):
        part = rows_of(z, j, y * 32, 32)
        return copy(part, part, s1s.at[k], s1r.at[z], (4 * (z + k) + j, head))

    for k in range(1, NZ):
        @pl.when(z + k < NZ)
        def _():
            z_copy(k).start()

    def y_copy(zs, k):
        part = rows_of(zs, j, y * 32, 32)
        return copy(part, part, s2s.at[zs], s2r.at[zs], (ctx, 2 * ((y + k) % 4) + xh))

    def x_copies(zs):
        low = rows_of(zs, j, 0, 64)
        high = rows_of(zs, j, 64, 64)
        return (copy(low, low, s3s.at[zs], s3r.at[zs], x_up),
                copy(high, high, s3s.at[zs], s3r.at[zs], x_down))

    def core_copy(zs, member, send):
        part = rows_of(zs, member, 0, ROWS)
        return copy(part, part, send.at[zs], s4r.at[zs], core)

    def stage1(d):
        zs = z - d
        arrived(rows_of(zs, j, y * 32, 32), s1r.at[zs])
        for k in range(1, 4):
            y_copy(zs, k).start()

    def stage2(d, wait=True):
        zs = z - d
        if wait:
            arrived(rows_of(zs, j, 0, 96), s2r.at[zs])
        for each in x_copies(zs):
            each.start()
        core_copy(zs, j, s3s).start()

    def stage3(d):
        zs = z - d
        arrived(rows_of(zs, opp, 0, ROWS), s3r.at[zs])
        core_copy(zs, opp, s4s).start()

    def stage4(d):
        zs = z - d
        arrived(lat.at[zs, pl.ds(0, 2 * ROWS), :], s4r.at[zs])

    swap = copy(w_ref.at[pl.ds(al((1 - xh) * HALF, 16), HALF), :], ball.at[z, xh], sws, swr, over)

    def ring_up(u):
        part = ball.at[(z + NZ - u // 2) % NZ, (xh + u) % 2]
        return copy(part, part, brs, brr.at[u], z_up)

    def ring_down(u):
        part = ball.at[(z + u // 2) % NZ, (xh + u + u // 6) % 2]
        return copy(part, part, bls, blr.at[u], z_down)

    def pass_up(k):
        arrived(ball.at[(z + 7 - k // 2) % NZ, (xh + k) % 2], brr.at[k])

        @pl.when(k < 5)
        def _():
            ring_up(k + 2).start()

    def pass_down(k):
        arrived(ball.at[(z + 1 + k // 2) % NZ, (xh + k + k // 6) % 2], blr.at[k])

        @pl.when(k < 4)
        def _():
            ring_down(k + 2).start()

        @pl.when(k == 5)
        def _():
            ring_down(6).start()

    def forward(k):
        @pl.when(z < 4)
        def _():
            pass_down(k)
            pass_up(k)

        @pl.when(z >= 4)
        def _():
            pass_up(k)
            pass_down(k)

    def when_in(d, act):
        @pl.when(d <= z)
        def _():
            act(d)

    swap.start()
    stage2(0, wait=False)

    def absorb(h):
        lanes = slice(h * ROWS, (h + 1) * ROWS)
        qa = lax.dot_general(uk_ref[:, h * NOPE:(h + 1) * NOPE], q_ref[:, h * HD:h * HD + NOPE], NT,
                             preferred_element_type=jnp.float32)
        qt[:LATENT, lanes] = (qa * SCALE).astype(jnp.bfloat16)
        qr = q_ref[:, h * HD + NOPE:(h + 1) * HD].astype(jnp.float32) * SCALE
        qt[LATENT:LATENT + ROPE, lanes] = qr.T.astype(jnp.bfloat16)

    qt[LATENT + ROPE:, :] = jnp.zeros((WIDE - LATENT - ROPE, TOTAL), jnp.bfloat16)
    fetch[2].wait()
    fetch[3].wait()
    for h in range(HEADS):
        absorb(h)
    fetch[4].wait()
    uvt[...] = uv_ref[...].T
    for d in range(1, 4):
        when_in(d, stage1)
    for k in range(1, NZ):
        @pl.when(z + k < NZ)
        def _():
            z_copy(k).wait_send()
    ring_up(0).start()
    ring_down(0).start()
    arrived(ball.at[z, 1 - xh], swr)
    ring_up(1).start()
    ring_down(1).start()
    when_in(1, stage2)
    when_in(4, stage1)
    when_in(5, stage1)
    when_in(2, stage2)
    stage3(0)
    when_in(3, stage2)
    forward(0)

    def visit(zs, first, chunk=None):
        block = lat[zs]
        turned = block[:, :LATENT].T

        def score(c):
            s = jnp.dot(block, qt[:, c * CHUNK:(c + 1) * CHUNK], preferred_element_type=jnp.float32)
            if first:
                row = j * ROWS + lax.broadcasted_iota(jnp.int32, s.shape, 1) % ROWS
                s = jnp.where(row >= lax.broadcasted_iota(jnp.int32, s.shape, 0), s, -jnp.inf)
            return s

        def rest(s, c):
            lanes = slice(c * CHUNK, (c + 1) * CHUNK)
            m_new = jnp.max(s, axis=0, keepdims=True)
            if not first:
                m_old = m_ref[:, lanes]
                m_new = jnp.maximum(m_old, m_new)
                alpha = jnp.exp2(m_old - m_new)
            p = jnp.exp2(s - m_new)
            total = jnp.sum(p, axis=0, keepdims=True)
            part = jnp.dot(turned, p.astype(jnp.bfloat16), preferred_element_type=jnp.float32)
            m_ref[:, lanes] = m_new
            if first:
                l_ref[:, lanes] = total
                acc[:, lanes] = part
            else:
                l_ref[:, lanes] = l_ref[:, lanes] * alpha + total
                acc[:, lanes] = acc[:, lanes] * alpha + part

        if chunk is None:
            s = score(0)
            later = score(1)
            rest(s, 0)
            rest(later, 1)
        else:
            rest(score(chunk), chunk)

    def ahead(i):
        when_in(i + 6, stage1)
        when_in(i + 4, stage2)

    stage4(0)
    visit(z, True)
    when_in(1, stage3)
    ahead(0)

    @pl.loop(1, z)
    def _(i):
        when_in(i + 1, stage3)
        stage4(i)
        visit(z - i, False)
        ahead(i)

        @pl.when(jnp.where(z >= 5, (i == 2) | (i == 4), i % 2 == 1))
        def _():
            forward((i + 1) // 2)

    def last_visit(c):
        @pl.when(z >= 1)
        def _():
            if c == 0:
                stage4(z)
            visit(0, False, c)

    done = 1 + jnp.minimum(z, 4) // 2

    def piece(across, member, c, start=0, count=PART):
        return abuf.at[across, pl.ds(c * PART + start, count), pl.ds(al(member * ROWS, ROWS), ROWS)]

    def a_sends(c):
        part = piece(xh, j, c)
        return (copy(part, part, axs, axr.at[c, 0], x_up),
                copy(part, part, axs, axr.at[c, 1], x_down),
                copy(part, part, axs, acr, core))

    def a_from_down(c):
        part, half = piece(down_xh, opp, c), piece(down_xh, opp, c, 0, PART // 2)
        return (copy(half, half, ars, arr.at[c], x_up),
                copy(part, part, ars, acr, core))

    def a_from_up(c):
        part, half = piece(up_xh, opp, c), piece(up_xh, opp, c, PART // 2, PART // 2)
        return (copy(half, half, ars, arr.at[c], x_down),
                copy(part, part, ars, acr, core))

    def a_across(c):
        part = piece(1 - xh, j, c)
        return copy(part, part, ars, acr, core)

    for c in range(4):
        if c % 2 == 0:
            last_visit(c // 2)
        for h in range(c * 2, c * 2 + 2):
            lanes = slice(h * ROWS, (h + 1) * ROWS)
            o = (acc[:, lanes] / l_ref[:, lanes]).astype(jnp.bfloat16)
            a = jnp.dot(uvt[h * NOPE:(h + 1) * NOPE, :], o, preferred_element_type=jnp.float32)
            abuf[xh, h * NOPE:(h + 1) * NOPE, mine] = a.astype(jnp.bfloat16)
        for each in a_sends(c):
            each.start()
        if c == 1:
            forward(done)
    for c in range(4):
        arrived(piece(down_xh, opp, c), axr.at[c, 0])
        for each in a_from_down(c):
            each.start()
        arrived(piece(up_xh, opp, c), axr.at[c, 1])
        for each in a_from_up(c):
            each.start()

    forward(done + 1)

    for c in range(4):
        arrived(piece(1 - xh, j, c), arr.at[c])
        a_across(c).start()
    forward(done + 2)
    arrived(abuf.at[0], acr)

    def home(s):
        far = (s + 1) // 2
        return (z + NZ + far * (1 - 2 * (s % 2))) % NZ

    def c_copy(s, t):
        return copy(cbuf.at[s, t], rbuf.at[s, y], cs, cr.at[s], (ctx, 2 * t + xh))

    def each_copy(s, act):
        for t in range(4):
            @pl.when(t != y)
            def _():
                act(c_copy(s, t))

    def multiply(slots):
        ct = None
        for across in range(2):
            blocks = [ball[home(s), across] for s in slots]
            rows = jnp.concatenate(blocks, axis=0) if len(blocks) > 1 else blocks[0]
            part = jnp.dot(rows, abuf[across], preferred_element_type=jnp.float32)
            ct = part if ct is None else ct + part
        ct = ct.astype(jnp.bfloat16)
        for r, s in enumerate(slots):
            for t in range(4):
                cbuf[s, t] = ct[r * HALF:(r + 1) * HALF, t * ROWS:(t + 1) * ROWS]
            each_copy(s, lambda each: each.start())

    spot = fin.at[pl.ds(al((2 * j + xh) * HALF, HALF), HALF), :]

    def f_copy(s):
        return copy(fsrc.at[s], spot, fs, fr, (base + y, home(s)))

    def is_here(s):
        return (y == j) & (home(s) == head)

    def gather(s):
        arrived(rbuf.at[s, pl.ds(0, 3)], cr.at[s])
        total = cbuf[s, y].astype(jnp.float32)
        for k in range(1, 4):
            total = total + rbuf[s, (y + k) % 4].astype(jnp.float32)
        fsrc[s] = total.astype(jnp.bfloat16)
        here = is_here(s)

        @pl.when(here)
        def _():
            spot[...] = fsrc[s]

        @pl.when(jnp.logical_not(here))
        def _():
            f_copy(s).start()

    def reach(k):
        @pl.when(k >= done + 3)
        def _():
            forward(k)

    multiply([0])

    @pl.loop(1, 4)
    def _(g):
        reach(2 * g - 2)
        reach(2 * g - 1)
        multiply([2 * g - 1, 2 * g])

        @pl.when(g == 3)
        def _():
            for s in range(3):
                gather(s)

    reach(6)
    multiply([7])

    @pl.loop(3, NZ)
    def _(s):
        gather(s)

    @pl.when(j == y)
    def _():
        arrived(fin.at[pl.ds(0, 7 * HALF), :], fr)

    @pl.when(j != y)
    def _():
        arrived(fin, fr)

    out_ref[...] = fin[...]

    @pl.loop(0, z + 1)
    def _(zs):
        @pl.when(zs < z)
        def _():
            left(rows_of(zs, j, 0, 96), s2s.at[zs])
        left(lat.at[zs, pl.ds(0, 2 * ROWS), :], s3s.at[zs])
        left(rows_of(zs, opp, 0, ROWS), s4s.at[zs])

    swap.wait_send()

    left(ball.at[pl.ds(0, 7), 0], brs)
    left(ball.at[pl.ds(0, 7), 0], bls)

    left(abuf.at[0, pl.ds(0, 768), :], axs)
    left(abuf.at[0], ars)

    left(cbuf.at[:, pl.ds(0, 3)], cs)

    @pl.when(j == y)
    def _():
        left(fsrc.at[pl.ds(0, 7)], fs)

    @pl.when(j != y)
    def _():
        left(fsrc, fs)


def on_device(queries, compressed, latent_gain, w_uk, w_uv, w_out):
    dma = pltpu.SemaphoreType.DMA
    bf = jnp.bfloat16
    return pl.pallas_call(
        kernel,
        out_shape=jax.ShapeDtypeStruct((NZ * HALF, ROWS), bf),
        in_specs=[pl.BlockSpec(memory_space=pltpu.VMEM if n == 2 else pl.ANY) for n in range(6)],
        out_specs=pl.BlockSpec(memory_space=pltpu.VMEM),
        scratch_shapes=[
            pltpu.VMEM((ROWS, HEADS * HD), bf),
            pltpu.VMEM((LATENT + ROPE, ROWS), bf),
            pltpu.VMEM((LATENT, HEADS * NOPE), bf),
            pltpu.VMEM((LATENT, HEADS * NOPE), bf),
            pltpu.VMEM((2 * HALF, HEADS * NOPE), bf),
            dma((5,)),
            pltpu.VMEM((NZ, STRIP, WIDE), bf),
            pltpu.VMEM((NZ, 2, HALF, HEADS * NOPE), bf),
            pltpu.VMEM((WIDE, TOTAL), bf),
            pltpu.VMEM((HEADS * NOPE, LATENT), bf),
            pltpu.VMEM((1, TOTAL), jnp.float32),
            pltpu.VMEM((1, TOTAL), jnp.float32),
            pltpu.VMEM((LATENT, TOTAL), jnp.float32),
            pltpu.VMEM((2, HEADS * NOPE, STRIP), bf),
            pltpu.VMEM((NZ, 4, HALF, ROWS), bf),
            pltpu.VMEM((NZ, 4, HALF, ROWS), bf),
            pltpu.VMEM((NZ, HALF, ROWS), bf),
            pltpu.VMEM((NZ * HALF, ROWS), bf),
            dma((NZ,)), dma((NZ,)),
            dma((NZ,)), dma((NZ,)),
            dma((NZ,)), dma((NZ,)),
            dma((NZ,)), dma((NZ,)),
            dma, dma,
            dma, dma((7,)),
            dma, dma((7,)),
            dma, dma((4, 2)),
            dma, dma((4,)), dma,
            dma, dma((NZ,)),
            dma, dma,
        ],
        compiler_params=pltpu.CompilerParams(
            collective_id=0, has_side_effects=True, vmem_limit_bytes=56 * 1024 * 1024),
        name="layer",
    )(queries, compressed.T, latent_gain.reshape(1, LATENT), w_uk, w_uv, w_out.T).T


def solution(mesh):
    return jax.shard_map(
        on_device,
        mesh=mesh,
        in_specs=(
            P("ctx", "head"),
            P("ctx", None),
            P(),
            P(None, "head"),
            P(None, "head"),
            P("head", "ctx"),
        ),
        out_specs=P("ctx", "head"),
        check_vma=False,
    )
```

```python
import math

import jax
import jax.numpy as jnp
from jax import lax
from jax.experimental import pallas as pl
from jax.experimental.pallas import tpu as pltpu
from jax.sharding import PartitionSpec as P

LATENT = 512
ROPE = 64
NOPE = 128
HD = NOPE + ROPE
WIDE = 640
ROWS = 128
HEADS = 8
STRIP = 4 * ROWS
TOTAL = HEADS * ROWS
CHUNK = 512
PART = 256
HALF = 112
NZ = 8
SCALE = HD ** -0.5 * math.log2(math.e)
NT = (((1,), (1,)), ((), ()))
MESH = pl.DeviceIdType.MESH


def al(value, unit):
    return pl.multiple_of(value, unit)


def kernel(q_hbm, comp_hbm, gain_ref, uk_hbm, uv_hbm, w_hbm, out_ref,
           q_ref, comp_ref, uk_ref, uv_ref, w_ref, loads,
           lat, ball, qt, uvt, m_ref, l_ref, acc, abuf, cbuf, rbuf, fsrc, fin,
           s1s, s1r, s2s, s2r, s3s, s3r, s4s, s4r, sws, swr, brs, brr, bls, blr,
           axs, axr, ars, arr, acr, cs, cr, fs, fr):
    ctx = lax.axis_index("ctx")
    head = lax.axis_index("head")
    z = ctx // 4
    j = ctx % 4
    y = head // 2
    xh = head % 2
    xl = j // 2
    base = 4 * z
    sib = j + 1 - 2 * (j % 2)
    opp = (j + 2) % 4
    opp_sib = (sib + 2) % 4
    up_xh = (xh + xl) % 2
    down_xh = 1 - up_xh
    over = (ctx, 2 * y + 1 - xh)
    core = (base + sib, head)
    x_up = (base + opp, 2 * y + up_xh)
    x_down = (base + opp, 2 * y + down_xh)
    z_up = (4 * ((z + 1) % NZ) + j, head)
    z_down = (4 * ((z + 7) % NZ) + j, head)

    def copy(src, dst, send, recv, device):
        return pltpu.make_async_remote_copy(
            src_ref=src, dst_ref=dst, send_sem=send, recv_sem=recv, device_id=device, device_id_type=MESH)

    def arrived(dst, recv):
        copy(dst, dst, recv, recv, core).wait_recv()

    def left(src, send):
        copy(src, src, send, send, core).wait_send()

    fetch = [pltpu.make_async_copy(a, b, loads.at[n]) for n, (a, b) in enumerate((
        (comp_hbm, comp_ref), (w_hbm, w_ref), (q_hbm, q_ref), (uk_hbm, uk_ref), (uv_hbm, uv_ref)))]
    for each in fetch:
        each.start()

    barrier = pltpu.get_barrier_semaphore()

    def greet(device):
        pl.semaphore_signal(barrier, inc=1, device_id=device, device_id_type=MESH)

    for k in range(1, NZ):
        greet((4 * ((z + k) % NZ) + j, head))
    for k in range(1, 4):
        greet((ctx, 2 * ((y + k) % 4) + xh))
    greet(over)
    greet(x_up)
    greet(x_down)
    greet(core)
    for p in range(4):
        for b in range(2):
            @pl.when((p != j) | (j != y) | (b != xh))
            def _():
                greet((base + p, 2 * j + b))

    fetch[0].wait()
    comp = comp_ref[...].T
    own = comp[:, :LATENT].astype(jnp.float32)
    mean_square = jnp.mean(own * own, axis=1, keepdims=True)
    normed = (own * lax.rsqrt(mean_square + 1e-06) * gain_ref[...]).astype(jnp.bfloat16)
    mine = pl.ds(al(j * ROWS, ROWS), ROWS)
    lat[z, mine, :LATENT] = normed
    lat[z, mine, LATENT:] = jnp.concatenate(
        [comp[:, LATENT:], jnp.zeros((ROWS, WIDE - LATENT - ROPE), jnp.bfloat16)], axis=1)
    fetch[1].wait()
    ball[z, xh] = w_ref[pl.ds(al(xh * HALF, 16), HALF), :]

    pl.semaphore_wait(barrier, jnp.where(j == y, 21, 22))

    def rows_of(zs, member, start, count):
        return lat.at[zs, pl.ds(al(member * ROWS + start, 16), count), :]

    def z_copy(k):
        part = rows_of(z, j, y * 32, 32)
        return copy(part, part, s1s.at[k], s1r.at[z], (4 * (z + k) + j, head))

    for k in range(1, NZ):
        @pl.when(z + k < NZ)
        def _():
            z_copy(k).start()

    def y_copy(zs, k):
        part = rows_of(zs, j, y * 32, 32)
        return copy(part, part, s2s.at[zs], s2r.at[zs], (ctx, 2 * ((y + k) % 4) + xh))

    def x_copies(zs):
        low = rows_of(zs, j, 0, 64)
        high = rows_of(zs, j, 64, 64)
        return (copy(low, low, s3s.at[zs], s3r.at[zs], x_up),
                copy(high, high, s3s.at[zs], s3r.at[zs], x_down))

    def core_copy(zs, member, send):
        part = rows_of(zs, member, 0, ROWS)
        return copy(part, part, send.at[zs], s4r.at[zs], core)

    def stage1(d):
        zs = z - d
        arrived(rows_of(zs, j, y * 32, 32), s1r.at[zs])
        for k in range(1, 4):
            y_copy(zs, k).start()

    def stage2(d, wait=True):
        zs = z - d
        if wait:
            arrived(rows_of(zs, j, 0, 96), s2r.at[zs])
        for each in x_copies(zs):
            each.start()
        core_copy(zs, j, s3s).start()

    def stage3(d):
        zs = z - d
        arrived(rows_of(zs, opp, 0, ROWS), s3r.at[zs])
        core_copy(zs, opp, s4s).start()

    def stage4(d):
        zs = z - d
        arrived(lat.at[zs, pl.ds(0, 2 * ROWS), :], s4r.at[zs])

    swap = copy(w_ref.at[pl.ds(al((1 - xh) * HALF, 16), HALF), :], ball.at[z, xh], sws, swr, over)

    def ring_up(u):
        part = ball.at[(z + NZ - u // 2) % NZ, (xh + u) % 2]
        return copy(part, part, brs, brr.at[u], z_up)

    def ring_down(u):
        part = ball.at[(z + u // 2) % NZ, (xh + u + u // 6) % 2]
        return copy(part, part, bls, blr.at[u], z_down)

    def pass_up(k):
        arrived(ball.at[(z + 7 - k // 2) % NZ, (xh + k) % 2], brr.at[k])

        @pl.when(k < 5)
        def _():
            ring_up(k + 2).start()

    def pass_down(k):
        arrived(ball.at[(z + 1 + k // 2) % NZ, (xh + k + k // 6) % 2], blr.at[k])

        @pl.when(k < 4)
        def _():
            ring_down(k + 2).start()

        @pl.when(k == 5)
        def _():
            ring_down(6).start()

    def forward(k):
        @pl.when(z < 4)
        def _():
            pass_down(k)
            pass_up(k)

        @pl.when(z >= 4)
        def _():
            pass_up(k)
            pass_down(k)

    def when_in(d, act):
        @pl.when(d <= z)
        def _():
            act(d)

    swap.start()
    stage2(0, wait=False)

    def absorb(h):
        lanes = slice(h * ROWS, (h + 1) * ROWS)
        qa = lax.dot_general(uk_ref[:, h * NOPE:(h + 1) * NOPE], q_ref[:, h * HD:h * HD + NOPE], NT,
                             preferred_element_type=jnp.float32)
        qt[:LATENT, lanes] = (qa * SCALE).astype(jnp.bfloat16)
        qr = q_ref[:, h * HD + NOPE:(h + 1) * HD].astype(jnp.float32) * SCALE
        qt[LATENT:LATENT + ROPE, lanes] = qr.T.astype(jnp.bfloat16)

    qt[LATENT + ROPE:, :] = jnp.zeros((WIDE - LATENT - ROPE, TOTAL), jnp.bfloat16)
    fetch[2].wait()
    fetch[3].wait()
    for h in range(HEADS):
        absorb(h)
    fetch[4].wait()
    uvt[...] = uv_ref[...].T
    for d in range(1, 4):
        when_in(d, stage1)
    for k in range(1, NZ):
        @pl.when(z + k < NZ)
        def _():
            z_copy(k).wait_send()
    ring_up(0).start()
    ring_down(0).start()
    stage3(0)
    arrived(ball.at[z, 1 - xh], swr)
    ring_up(1).start()
    ring_down(1).start()
    when_in(4, stage1)
    when_in(5, stage1)
    when_in(1, stage2)

    def visit(zs, first, chunk=None):
        block = lat[zs]
        turned = block[:, :LATENT].T

        def score(c):
            s = jnp.dot(block, qt[:, c * CHUNK:(c + 1) * CHUNK], preferred_element_type=jnp.float32)
            if first:
                row = j * ROWS + lax.broadcasted_iota(jnp.int32, s.shape, 1) % ROWS
                s = jnp.where(row >= lax.broadcasted_iota(jnp.int32, s.shape, 0), s, -jnp.inf)
            return s

        def rest(s, c):
            lanes = slice(c * CHUNK, (c + 1) * CHUNK)
            m_new = jnp.max(s, axis=0, keepdims=True)
            if not first:
                m_old = m_ref[:, lanes]
                m_new = jnp.maximum(m_old, m_new)
                alpha = jnp.exp2(m_old - m_new)
            p = jnp.exp2(s - m_new)
            total = jnp.sum(p, axis=0, keepdims=True)
            part = jnp.dot(turned, p.astype(jnp.bfloat16), preferred_element_type=jnp.float32)
            m_ref[:, lanes] = m_new
            if first:
                l_ref[:, lanes] = total
                acc[:, lanes] = part
            else:
                l_ref[:, lanes] = l_ref[:, lanes] * alpha + total
                acc[:, lanes] = acc[:, lanes] * alpha + part

        if chunk is None:
            s = score(0)
            later = score(1)
            rest(s, 0)
            rest(later, 1)
        else:
            rest(score(chunk), chunk)

    stage4(0)
    visit(z, True)
    when_in(2, stage2)
    when_in(6, stage1)
    when_in(3, stage2)
    when_in(1, stage3)
    forward(0)

    @pl.loop(1, z)
    def _(i):
        when_in(i + 1, stage3)
        when_in(i + 6, stage1)
        when_in(i + 3, stage2)
        stage4(i)
        visit(z - i, False)

        @pl.when(jnp.where(z >= 5, (i == 2) | (i == 4), i % 2 == 1))
        def _():
            forward((i + 1) // 2)

    def last_visit(c):
        @pl.when(z >= 1)
        def _():
            if c == 0:
                stage4(z)
            visit(0, False, c)

    done = 1 + jnp.minimum(z, 4) // 2

    def piece(across, member, c, start=0, count=PART):
        return abuf.at[across, pl.ds(c * PART + start, count), pl.ds(al(member * ROWS, ROWS), ROWS)]

    def a_sends(c):
        part = piece(xh, j, c)
        return (copy(part, part, axs, axr.at[c, 0], x_up),
                copy(part, part, axs, axr.at[c, 1], x_down),
                copy(part, part, axs, acr, core))

    def a_from_down(c):
        part, half = piece(down_xh, opp, c), piece(down_xh, opp, c, 0, PART // 2)
        return (copy(half, half, ars, arr.at[c], x_up),
                copy(part, part, ars, acr, core))

    def a_from_up(c):
        part, half = piece(up_xh, opp, c), piece(up_xh, opp, c, PART // 2, PART // 2)
        return (copy(half, half, ars, arr.at[c], x_down),
                copy(part, part, ars, acr, core))

    def a_across(c):
        part = piece(1 - xh, j, c)
        return copy(part, part, ars, acr, core)

    for c in range(4):
        if c % 2 == 0:
            last_visit(c // 2)
        for h in range(c * 2, c * 2 + 2):
            lanes = slice(h * ROWS, (h + 1) * ROWS)
            o = (acc[:, lanes] / l_ref[:, lanes]).astype(jnp.bfloat16)
            a = jnp.dot(uvt[h * NOPE:(h + 1) * NOPE, :], o, preferred_element_type=jnp.float32)
            abuf[xh, h * NOPE:(h + 1) * NOPE, mine] = a.astype(jnp.bfloat16)
        for each in a_sends(c):
            each.start()
        if c == 1:
            forward(done)
    for c in range(4):
        arrived(piece(down_xh, opp, c), axr.at[c, 0])
        for each in a_from_down(c):
            each.start()
        arrived(piece(up_xh, opp, c), axr.at[c, 1])
        for each in a_from_up(c):
            each.start()

    forward(done + 1)

    for c in range(4):
        arrived(piece(1 - xh, j, c), arr.at[c])
        a_across(c).start()
    forward(done + 2)
    arrived(abuf.at[0], acr)

    def home(s):
        far = (s + 1) // 2
        return (z + NZ + far * (1 - 2 * (s % 2))) % NZ

    def c_copy(s, t):
        return copy(cbuf.at[s, t], rbuf.at[s, y], cs, cr.at[s], (ctx, 2 * t + xh))

    def each_copy(s, act):
        for t in range(4):
            @pl.when(t != y)
            def _():
                act(c_copy(s, t))

    def multiply(slots):
        ct = None
        for across in range(2):
            blocks = [ball[home(s), across] for s in slots]
            rows = jnp.concatenate(blocks, axis=0) if len(blocks) > 1 else blocks[0]
            part = jnp.dot(rows, abuf[across], preferred_element_type=jnp.float32)
            ct = part if ct is None else ct + part
        ct = ct.astype(jnp.bfloat16)
        for r, s in enumerate(slots):
            for t in range(4):
                cbuf[s, t] = ct[r * HALF:(r + 1) * HALF, t * ROWS:(t + 1) * ROWS]
            each_copy(s, lambda each: each.start())

    spot = fin.at[pl.ds(al((2 * j + xh) * HALF, HALF), HALF), :]

    def f_copy(s):
        return copy(fsrc.at[s], spot, fs, fr, (base + y, home(s)))

    def is_here(s):
        return (y == j) & (home(s) == head)

    def gather(s):
        arrived(rbuf.at[s, pl.ds(0, 3)], cr.at[s])
        total = cbuf[s, y].astype(jnp.float32)
        for k in range(1, 4):
            total = total + rbuf[s, (y + k) % 4].astype(jnp.float32)
        fsrc[s] = total.astype(jnp.bfloat16)
        here = is_here(s)

        @pl.when(here)
        def _():
            spot[...] = fsrc[s]

        @pl.when(jnp.logical_not(here))
        def _():
            f_copy(s).start()

    def reach(k):
        @pl.when(k >= done + 3)
        def _():
            forward(k)

    multiply([0])

    @pl.loop(1, 4)
    def _(g):
        reach(2 * g - 2)
        reach(2 * g - 1)
        multiply([2 * g - 1, 2 * g])

        @pl.when(g == 3)
        def _():
            for s in range(3):
                gather(s)

    reach(6)
    multiply([7])

    @pl.loop(3, NZ)
    def _(s):
        gather(s)

    @pl.when(j == y)
    def _():
        arrived(fin.at[pl.ds(0, 7 * HALF), :], fr)

    @pl.when(j != y)
    def _():
        arrived(fin, fr)

    out_ref[...] = fin[...]

    @pl.loop(0, z + 1)
    def _(zs):
        @pl.when(zs < z)
        def _():
            left(rows_of(zs, j, 0, 96), s2s.at[zs])
        left(lat.at[zs, pl.ds(0, 2 * ROWS), :], s3s.at[zs])
        left(rows_of(zs, opp, 0, ROWS), s4s.at[zs])

    swap.wait_send()

    left(ball.at[pl.ds(0, 7), 0], brs)
    left(ball.at[pl.ds(0, 7), 0], bls)

    left(abuf.at[0, pl.ds(0, 768), :], axs)
    left(abuf.at[0], ars)

    left(cbuf.at[:, pl.ds(0, 3)], cs)

    @pl.when(j == y)
    def _():
        left(fsrc.at[pl.ds(0, 7)], fs)

    @pl.when(j != y)
    def _():
        left(fsrc, fs)


def on_device(queries, compressed, latent_gain, w_uk, w_uv, w_out):
    dma = pltpu.SemaphoreType.DMA
    bf = jnp.bfloat16
    return pl.pallas_call(
        kernel,
        out_shape=jax.ShapeDtypeStruct((NZ * HALF, ROWS), bf),
        in_specs=[pl.BlockSpec(memory_space=pltpu.VMEM if n == 2 else pl.ANY) for n in range(6)],
        out_specs=pl.BlockSpec(memory_space=pltpu.VMEM),
        scratch_shapes=[
            pltpu.VMEM((ROWS, HEADS * HD), bf),
            pltpu.VMEM((LATENT + ROPE, ROWS), bf),
            pltpu.VMEM((LATENT, HEADS * NOPE), bf),
            pltpu.VMEM((LATENT, HEADS * NOPE), bf),
            pltpu.VMEM((2 * HALF, HEADS * NOPE), bf),
            dma((5,)),
            pltpu.VMEM((NZ, STRIP, WIDE), bf),
            pltpu.VMEM((NZ, 2, HALF, HEADS * NOPE), bf),
            pltpu.VMEM((WIDE, TOTAL), bf),
            pltpu.VMEM((HEADS * NOPE, LATENT), bf),
            pltpu.VMEM((1, TOTAL), jnp.float32),
            pltpu.VMEM((1, TOTAL), jnp.float32),
            pltpu.VMEM((LATENT, TOTAL), jnp.float32),
            pltpu.VMEM((2, HEADS * NOPE, STRIP), bf),
            pltpu.VMEM((NZ, 4, HALF, ROWS), bf),
            pltpu.VMEM((NZ, 4, HALF, ROWS), bf),
            pltpu.VMEM((NZ, HALF, ROWS), bf),
            pltpu.VMEM((NZ * HALF, ROWS), bf),
            dma((NZ,)), dma((NZ,)),
            dma((NZ,)), dma((NZ,)),
            dma((NZ,)), dma((NZ,)),
            dma((NZ,)), dma((NZ,)),
            dma, dma,
            dma, dma((7,)),
            dma, dma((7,)),
            dma, dma((4, 2)),
            dma, dma((4,)), dma,
            dma, dma((NZ,)),
            dma, dma,
        ],
        compiler_params=pltpu.CompilerParams(
            collective_id=0, has_side_effects=True, vmem_limit_bytes=56 * 1024 * 1024),
        name="layer",
    )(queries, compressed.T, latent_gain.reshape(1, LATENT), w_uk, w_uv, w_out.T).T


def solution(mesh):
    return jax.shard_map(
        on_device,
        mesh=mesh,
        in_specs=(
            P("ctx", "head"),
            P("ctx", None),
            P(),
            P(None, "head"),
            P(None, "head"),
            P("head", "ctx"),
        ),
        out_specs=P("ctx", "head"),
        check_vma=False,
    )
```

```python
import math

import jax
import jax.numpy as jnp
from jax import lax
from jax.experimental import pallas as pl
from jax.experimental.pallas import tpu as pltpu
from jax.sharding import PartitionSpec as P

LATENT = 512
ROPE = 64
NOPE = 128
HD = NOPE + ROPE
WIDE = 640
ROWS = 128
HEADS = 8
STRIP = 4 * ROWS
TOTAL = HEADS * ROWS
CHUNK = 512
PART = 256
HALF = 112
NZ = 8
SCALE = HD ** -0.5 * math.log2(math.e)
NT = (((1,), (1,)), ((), ()))
MESH = pl.DeviceIdType.MESH


def al(value, unit):
    return pl.multiple_of(value, unit)


def kernel(q_hbm, comp_hbm, gain_ref, uk_hbm, uv_hbm, w_hbm, out_ref,
           q_ref, comp_ref, uk_ref, uv_ref, w_ref, loads,
           lat, ball, qt, uvt, m_ref, l_ref, acc, abuf, cbuf, rbuf, fsrc, fin,
           s1s, s1r, s2s, s2r, s3s, s3r, s4s, s4r, sws, swr, brs, brr, bls, blr,
           axs, axr, ars, arr, acr, cs, cr, fs, fr):
    ctx = lax.axis_index("ctx")
    head = lax.axis_index("head")
    z = ctx // 4
    j = ctx % 4
    y = head // 2
    xh = head % 2
    xl = j // 2
    base = 4 * z
    sib = j + 1 - 2 * (j % 2)
    opp = (j + 2) % 4
    opp_sib = (sib + 2) % 4
    up_xh = (xh + xl) % 2
    down_xh = 1 - up_xh
    over = (ctx, 2 * y + 1 - xh)
    core = (base + sib, head)
    x_up = (base + opp, 2 * y + up_xh)
    x_down = (base + opp, 2 * y + down_xh)
    z_up = (4 * ((z + 1) % NZ) + j, head)
    z_down = (4 * ((z + 7) % NZ) + j, head)

    def copy(src, dst, send, recv, device):
        return pltpu.make_async_remote_copy(
            src_ref=src, dst_ref=dst, send_sem=send, recv_sem=recv, device_id=device, device_id_type=MESH)

    def arrived(dst, recv):
        copy(dst, dst, recv, recv, core).wait_recv()

    def left(src, send):
        copy(src, src, send, send, core).wait_send()

    fetch = [pltpu.make_async_copy(a, b, loads.at[n]) for n, (a, b) in enumerate((
        (comp_hbm, comp_ref), (w_hbm, w_ref), (q_hbm, q_ref), (uk_hbm, uk_ref), (uv_hbm, uv_ref)))]
    for each in fetch:
        each.start()

    barrier = pltpu.get_barrier_semaphore()

    def greet(device):
        pl.semaphore_signal(barrier, inc=1, device_id=device, device_id_type=MESH)

    for k in range(1, NZ):
        greet((4 * ((z + k) % NZ) + j, head))
    for k in range(1, 4):
        greet((ctx, 2 * ((y + k) % 4) + xh))
    greet(over)
    greet(x_up)
    greet(x_down)
    greet(core)
    for p in range(4):
        for b in range(2):
            @pl.when((p != j) | (j != y) | (b != xh))
            def _():
                greet((base + p, 2 * j + b))

    fetch[0].wait()
    comp = comp_ref[...].T
    own = comp[:, :LATENT].astype(jnp.float32)
    mean_square = jnp.mean(own * own, axis=1, keepdims=True)
    normed = (own * lax.rsqrt(mean_square + 1e-06) * gain_ref[...]).astype(jnp.bfloat16)
    mine = pl.ds(al(j * ROWS, ROWS), ROWS)
    lat[z, mine, :LATENT] = normed
    lat[z, mine, LATENT:] = jnp.concatenate(
        [comp[:, LATENT:], jnp.zeros((ROWS, WIDE - LATENT - ROPE), jnp.bfloat16)], axis=1)
    fetch[1].wait()
    ball[z, xh] = w_ref[pl.ds(al(xh * HALF, 16), HALF), :]

    pl.semaphore_wait(barrier, jnp.where(j == y, 21, 22))

    def rows_of(zs, member, start, count):
        return lat.at[zs, pl.ds(al(member * ROWS + start, 16), count), :]

    def z_copy(k):
        part = rows_of(z, j, y * 32, 32)
        return copy(part, part, s1s.at[k], s1r.at[z], (4 * (z + k) + j, head))

    for k in range(1, NZ):
        @pl.when(z + k < NZ)
        def _():
            z_copy(k).start()

    def y_copy(zs, k):
        part = rows_of(zs, j, y * 32, 32)
        return copy(part, part, s2s.at[zs], s2r.at[zs], (ctx, 2 * ((y + k) % 4) + xh))

    def x_copies(zs):
        low = rows_of(zs, j, 0, 64)
        high = rows_of(zs, j, 64, 64)
        return (copy(low, low, s3s.at[zs], s3r.at[zs], x_up),
                copy(high, high, s3s.at[zs], s3r.at[zs], x_down))

    def core_copy(zs, member, send):
        part = rows_of(zs, member, 0, ROWS)
        return copy(part, part, send.at[zs], s4r.at[zs], core)

    def stage1(d):
        zs = z - d
        arrived(rows_of(zs, j, y * 32, 32), s1r.at[zs])
        for k in range(1, 4):
            y_copy(zs, k).start()

    def stage2(d, wait=True):
        zs = z - d
        if wait:
            arrived(rows_of(zs, j, 0, 96), s2r.at[zs])
        for each in x_copies(zs):
            each.start()
        core_copy(zs, j, s3s).start()

    def stage3(d):
        zs = z - d
        arrived(rows_of(zs, opp, 0, ROWS), s3r.at[zs])
        core_copy(zs, opp, s4s).start()

    def stage4(d):
        zs = z - d
        arrived(lat.at[zs, pl.ds(0, 2 * ROWS), :], s4r.at[zs])

    swap = copy(w_ref.at[pl.ds(al((1 - xh) * HALF, 16), HALF), :], ball.at[z, xh], sws, swr, over)

    def ring_up(u):
        part = ball.at[(z + NZ - u // 2) % NZ, (xh + u) % 2]
        return copy(part, part, brs, brr.at[u], z_up)

    def ring_down(u):
        part = ball.at[(z + u // 2) % NZ, (xh + u + u // 6) % 2]
        return copy(part, part, bls, blr.at[u], z_down)

    def pass_up(k):
        arrived(ball.at[(z + 7 - k // 2) % NZ, (xh + k) % 2], brr.at[k])

        @pl.when(k < 5)
        def _():
            ring_up(k + 2).start()

    def pass_down(k):
        arrived(ball.at[(z + 1 + k // 2) % NZ, (xh + k + k // 6) % 2], blr.at[k])

        @pl.when(k < 4)
        def _():
            ring_down(k + 2).start()

        @pl.when(k == 5)
        def _():
            ring_down(6).start()

    def forward(k):
        @pl.when(z < 4)
        def _():
            pass_down(k)
            pass_up(k)

        @pl.when(z >= 4)
        def _():
            pass_up(k)
            pass_down(k)

    def when_in(d, act):
        @pl.when(d <= z)
        def _():
            act(d)

    swap.start()
    stage2(0, wait=False)
    ring_up(0).start()
    ring_down(0).start()

    def absorb(h):
        lanes = slice(h * ROWS, (h + 1) * ROWS)
        qa = lax.dot_general(uk_ref[:, h * NOPE:(h + 1) * NOPE], q_ref[:, h * HD:h * HD + NOPE], NT,
                             preferred_element_type=jnp.float32)
        qt[:LATENT, lanes] = (qa * SCALE).astype(jnp.bfloat16)
        qr = q_ref[:, h * HD + NOPE:(h + 1) * HD].astype(jnp.float32) * SCALE
        qt[LATENT:LATENT + ROPE, lanes] = qr.T.astype(jnp.bfloat16)

    qt[LATENT + ROPE:, :] = jnp.zeros((WIDE - LATENT - ROPE, TOTAL), jnp.bfloat16)
    fetch[2].wait()
    fetch[3].wait()
    for h in range(HEADS):
        absorb(h)
    fetch[4].wait()
    uvt[...] = uv_ref[...].T
    for d in range(1, 4):
        when_in(d, stage1)
    for k in range(1, NZ):
        @pl.when(z + k < NZ)
        def _():
            z_copy(k).wait_send()
    stage3(0)
    arrived(ball.at[z, 1 - xh], swr)
    ring_up(1).start()
    ring_down(1).start()
    when_in(4, stage1)
    when_in(5, stage1)
    when_in(1, stage2)

    def visit(zs, first, chunk=None):
        block = lat[zs]
        turned = block[:, :LATENT].T

        def score(c):
            s = jnp.dot(block, qt[:, c * CHUNK:(c + 1) * CHUNK], preferred_element_type=jnp.float32)
            if first:
                row = j * ROWS + lax.broadcasted_iota(jnp.int32, s.shape, 1) % ROWS
                s = jnp.where(row >= lax.broadcasted_iota(jnp.int32, s.shape, 0), s, -jnp.inf)
            return s

        def rest(s, c):
            lanes = slice(c * CHUNK, (c + 1) * CHUNK)
            m_new = jnp.max(s, axis=0, keepdims=True)
            if not first:
                m_old = m_ref[:, lanes]
                m_new = jnp.maximum(m_old, m_new)
                alpha = jnp.exp2(m_old - m_new)
            p = jnp.exp2(s - m_new)
            total = jnp.sum(p, axis=0, keepdims=True)
            part = jnp.dot(turned, p.astype(jnp.bfloat16), preferred_element_type=jnp.float32)
            m_ref[:, lanes] = m_new
            if first:
                l_ref[:, lanes] = total
                acc[:, lanes] = part
            else:
                l_ref[:, lanes] = l_ref[:, lanes] * alpha + total
                acc[:, lanes] = acc[:, lanes] * alpha + part

        if chunk is None:
            s = score(0)
            later = score(1)
            rest(s, 0)
            rest(later, 1)
        else:
            rest(score(chunk), chunk)

    stage4(0)
    visit(z, True)
    when_in(2, stage2)
    when_in(6, stage1)
    when_in(3, stage2)
    when_in(1, stage3)
    forward(0)

    @pl.loop(1, z)
    def _(i):
        when_in(i + 1, stage3)
        when_in(i + 6, stage1)
        when_in(i + 3, stage2)
        stage4(i)
        visit(z - i, False)

        @pl.when(jnp.where(z >= 5, (i == 2) | (i == 4), i % 2 == 1))
        def _():
            forward((i + 1) // 2)

    def last_visit(c):
        @pl.when(z >= 1)
        def _():
            if c == 0:
                stage4(z)
            visit(0, False, c)

    done = 1 + jnp.minimum(z, 4) // 2

    def piece(across, member, c, start=0, count=PART):
        return abuf.at[across, pl.ds(c * PART + start, count), pl.ds(al(member * ROWS, ROWS), ROWS)]

    def a_sends(c):
        part = piece(xh, j, c)
        return (copy(part, part, axs, axr.at[c, 0], x_up),
                copy(part, part, axs, axr.at[c, 1], x_down),
                copy(part, part, axs, acr, core))

    def a_from_down(c):
        part, half = piece(down_xh, opp, c), piece(down_xh, opp, c, 0, PART // 2)
        return (copy(half, half, ars, arr.at[c], x_up),
                copy(part, part, ars, acr, core))

    def a_from_up(c):
        part, half = piece(up_xh, opp, c), piece(up_xh, opp, c, PART // 2, PART // 2)
        return (copy(half, half, ars, arr.at[c], x_down),
                copy(part, part, ars, acr, core))

    def a_across(c):
        part = piece(1 - xh, j, c)
        return copy(part, part, ars, acr, core)

    for c in range(4):
        if c % 2 == 0:
            last_visit(c // 2)
        for h in range(c * 2, c * 2 + 2):
            lanes = slice(h * ROWS, (h + 1) * ROWS)
            o = (acc[:, lanes] / l_ref[:, lanes]).astype(jnp.bfloat16)
            a = jnp.dot(uvt[h * NOPE:(h + 1) * NOPE, :], o, preferred_element_type=jnp.float32)
            abuf[xh, h * NOPE:(h + 1) * NOPE, mine] = a.astype(jnp.bfloat16)
        for each in a_sends(c):
            each.start()
        if c == 1:
            forward(done)
    for c in range(4):
        arrived(piece(down_xh, opp, c), axr.at[c, 0])
        for each in a_from_down(c):
            each.start()
        arrived(piece(up_xh, opp, c), axr.at[c, 1])
        for each in a_from_up(c):
            each.start()

    forward(done + 1)

    for c in range(4):
        arrived(piece(1 - xh, j, c), arr.at[c])
        a_across(c).start()
    forward(done + 2)
    arrived(abuf.at[0], acr)

    def home(s):
        far = (s + 1) // 2
        return (z + NZ + far * (1 - 2 * (s % 2))) % NZ

    def c_copy(s, t):
        return copy(cbuf.at[s, t], rbuf.at[s, y], cs, cr.at[s], (ctx, 2 * t + xh))

    def each_copy(s, act):
        for t in range(4):
            @pl.when(t != y)
            def _():
                act(c_copy(s, t))

    def multiply(slots):
        ct = None
        for across in range(2):
            blocks = [ball[home(s), across] for s in slots]
            rows = jnp.concatenate(blocks, axis=0) if len(blocks) > 1 else blocks[0]
            part = jnp.dot(rows, abuf[across], preferred_element_type=jnp.float32)
            ct = part if ct is None else ct + part
        ct = ct.astype(jnp.bfloat16)
        for r, s in enumerate(slots):
            for t in range(4):
                cbuf[s, t] = ct[r * HALF:(r + 1) * HALF, t * ROWS:(t + 1) * ROWS]
            each_copy(s, lambda each: each.start())

    spot = fin.at[pl.ds(al((2 * j + xh) * HALF, HALF), HALF), :]

    def f_copy(s):
        return copy(fsrc.at[s], spot, fs, fr, (base + y, home(s)))

    def is_here(s):
        return (y == j) & (home(s) == head)

    def gather(s):
        arrived(rbuf.at[s, pl.ds(0, 3)], cr.at[s])
        total = cbuf[s, y].astype(jnp.float32)
        for k in range(1, 4):
            total = total + rbuf[s, (y + k) % 4].astype(jnp.float32)
        fsrc[s] = total.astype(jnp.bfloat16)
        here = is_here(s)

        @pl.when(here)
        def _():
            spot[...] = fsrc[s]

        @pl.when(jnp.logical_not(here))
        def _():
            f_copy(s).start()

    def reach(k):
        @pl.when(k >= done + 3)
        def _():
            forward(k)

    multiply([0])

    @pl.loop(1, 4)
    def _(g):
        reach(2 * g - 2)
        reach(2 * g - 1)
        multiply([2 * g - 1, 2 * g])

        @pl.when(g == 3)
        def _():
            for s in range(3):
                gather(s)

    reach(6)
    multiply([7])

    @pl.loop(3, NZ)
    def _(s):
        gather(s)

    @pl.when(j == y)
    def _():
        arrived(fin.at[pl.ds(0, 7 * HALF), :], fr)

    @pl.when(j != y)
    def _():
        arrived(fin, fr)

    out_ref[...] = fin[...]

    @pl.loop(0, z + 1)
    def _(zs):
        @pl.when(zs < z)
        def _():
            left(rows_of(zs, j, 0, 96), s2s.at[zs])
        left(lat.at[zs, pl.ds(0, 2 * ROWS), :], s3s.at[zs])
        left(rows_of(zs, opp, 0, ROWS), s4s.at[zs])

    swap.wait_send()

    left(ball.at[pl.ds(0, 7), 0], brs)
    left(ball.at[pl.ds(0, 7), 0], bls)

    left(abuf.at[0, pl.ds(0, 768), :], axs)
    left(abuf.at[0], ars)

    left(cbuf.at[:, pl.ds(0, 3)], cs)

    @pl.when(j == y)
    def _():
        left(fsrc.at[pl.ds(0, 7)], fs)

    @pl.when(j != y)
    def _():
        left(fsrc, fs)


def on_device(queries, compressed, latent_gain, w_uk, w_uv, w_out):
    dma = pltpu.SemaphoreType.DMA
    bf = jnp.bfloat16
    return pl.pallas_call(
        kernel,
        out_shape=jax.ShapeDtypeStruct((NZ * HALF, ROWS), bf),
        in_specs=[pl.BlockSpec(memory_space=pltpu.VMEM if n == 2 else pl.ANY) for n in range(6)],
        out_specs=pl.BlockSpec(memory_space=pltpu.VMEM),
        scratch_shapes=[
            pltpu.VMEM((ROWS, HEADS * HD), bf),
            pltpu.VMEM((LATENT + ROPE, ROWS), bf),
            pltpu.VMEM((LATENT, HEADS * NOPE), bf),
            pltpu.VMEM((LATENT, HEADS * NOPE), bf),
            pltpu.VMEM((2 * HALF, HEADS * NOPE), bf),
            dma((5,)),
            pltpu.VMEM((NZ, STRIP, WIDE), bf),
            pltpu.VMEM((NZ, 2, HALF, HEADS * NOPE), bf),
            pltpu.VMEM((WIDE, TOTAL), bf),
            pltpu.VMEM((HEADS * NOPE, LATENT), bf),
            pltpu.VMEM((1, TOTAL), jnp.float32),
            pltpu.VMEM((1, TOTAL), jnp.float32),
            pltpu.VMEM((LATENT, TOTAL), jnp.float32),
            pltpu.VMEM((2, HEADS * NOPE, STRIP), bf),
            pltpu.VMEM((NZ, 4, HALF, ROWS), bf),
            pltpu.VMEM((NZ, 4, HALF, ROWS), bf),
            pltpu.VMEM((NZ, HALF, ROWS), bf),
            pltpu.VMEM((NZ * HALF, ROWS), bf),
            dma((NZ,)), dma((NZ,)),
            dma((NZ,)), dma((NZ,)),
            dma((NZ,)), dma((NZ,)),
            dma((NZ,)), dma((NZ,)),
            dma, dma,
            dma, dma((7,)),
            dma, dma((7,)),
            dma, dma((4, 2)),
            dma, dma((4,)), dma,
            dma, dma((NZ,)),
            dma, dma,
        ],
        compiler_params=pltpu.CompilerParams(
            collective_id=0, has_side_effects=True, vmem_limit_bytes=56 * 1024 * 1024),
        name="layer",
    )(queries, compressed.T, latent_gain.reshape(1, LATENT), w_uk, w_uv, w_out.T).T


def solution(mesh):
    return jax.shard_map(
        on_device,
        mesh=mesh,
        in_specs=(
            P("ctx", "head"),
            P("ctx", None),
            P(),
            P(None, "head"),
            P(None, "head"),
            P("head", "ctx"),
        ),
        out_specs=P("ctx", "head"),
        check_vma=False,
    )
```

```python
import math

import jax
import jax.numpy as jnp
from jax import lax
from jax.experimental import pallas as pl
from jax.experimental.pallas import tpu as pltpu
from jax.sharding import PartitionSpec as P

LATENT = 512
ROPE = 64
NOPE = 128
HD = NOPE + ROPE
WIDE = 640
ROWS = 128
HEADS = 8
STRIP = 4 * ROWS
TOTAL = HEADS * ROWS
CHUNK = 512
PART = 256
HALF = 112
NZ = 8
SCALE = HD ** -0.5 * math.log2(math.e)
NT = (((1,), (1,)), ((), ()))
MESH = pl.DeviceIdType.MESH


def al(value, unit):
    return pl.multiple_of(value, unit)


def kernel(q_hbm, comp_hbm, gain_ref, uk_hbm, uv_hbm, w_hbm, out_ref,
           q_ref, comp_ref, uk_ref, uv_ref, w_ref, loads,
           lat, ball, qt, uvt, m_ref, l_ref, acc, abuf, cbuf, rbuf, fsrc, fin,
           s1s, s1r, s2s, s2r, s3r, s4r, sws, swr, brs, brr, bls, blr,
           axs, axr, ars, arr, acr, cs, cr, fs, fr):
    ctx = lax.axis_index("ctx")
    head = lax.axis_index("head")
    z = ctx // 4
    j = ctx % 4
    y = head // 2
    xh = head % 2
    xl = j // 2
    base = 4 * z
    sib = j + 1 - 2 * (j % 2)
    opp = (j + 2) % 4
    opp_sib = (sib + 2) % 4
    up_xh = (xh + xl) % 2
    down_xh = 1 - up_xh
    over = (ctx, 2 * y + 1 - xh)
    core = (base + sib, head)
    x_up = (base + opp, 2 * y + up_xh)
    x_down = (base + opp, 2 * y + down_xh)
    z_up = (4 * ((z + 1) % NZ) + j, head)
    z_down = (4 * ((z + 7) % NZ) + j, head)

    def copy(src, dst, send, recv, device):
        return pltpu.make_async_remote_copy(
            src_ref=src, dst_ref=dst, send_sem=send, recv_sem=recv, device_id=device, device_id_type=MESH)

    def arrived(dst, recv):
        copy(dst, dst, recv, recv, core).wait_recv()

    def left(src, send):
        copy(src, src, send, send, core).wait_send()

    fetch = [pltpu.make_async_copy(a, b, loads.at[n]) for n, (a, b) in enumerate((
        (comp_hbm, comp_ref), (w_hbm, w_ref), (q_hbm, q_ref), (uk_hbm, uk_ref), (uv_hbm, uv_ref)))]
    for each in fetch:
        each.start()

    barrier = pltpu.get_barrier_semaphore()

    def greet(device):
        pl.semaphore_signal(barrier, inc=1, device_id=device, device_id_type=MESH)

    for k in range(1, NZ):
        greet((4 * ((z + k) % NZ) + j, head))
    for k in range(1, 4):
        greet((ctx, 2 * ((y + k) % 4) + xh))
    greet(over)
    greet(x_up)
    greet(x_down)
    greet(core)
    for p in range(4):
        for b in range(2):
            @pl.when((p != j) | (j != y) | (b != xh))
            def _():
                greet((base + p, 2 * j + b))

    fetch[0].wait()
    comp = comp_ref[...].T
    own = comp[:, :LATENT].astype(jnp.float32)
    mean_square = jnp.mean(own * own, axis=1, keepdims=True)
    normed = (own * lax.rsqrt(mean_square + 1e-06) * gain_ref[...]).astype(jnp.bfloat16)
    mine = pl.ds(al(j * ROWS, ROWS), ROWS)
    lat[z, mine, :LATENT] = normed
    lat[z, mine, LATENT:] = jnp.concatenate(
        [comp[:, LATENT:], jnp.zeros((ROWS, WIDE - LATENT - ROPE), jnp.bfloat16)], axis=1)
    fetch[1].wait()
    ball[z, xh] = w_ref[pl.ds(al(xh * HALF, 16), HALF), :]

    pl.semaphore_wait(barrier, jnp.where(j == y, 21, 22))

    def rows_of(zs, member, start, count):
        return lat.at[zs, pl.ds(al(member * ROWS + start, 16), count), :]

    def z_copy(k):
        part = rows_of(z, j, y * 32, 32)
        return copy(part, part, s1s.at[k], s1r.at[z], (4 * (z + k) + j, head))

    for k in range(1, NZ):
        @pl.when(z + k < NZ)
        def _():
            z_copy(k).start()

    def y_copy(zs, k):
        part = rows_of(zs, j, y * 32, 32)
        return copy(part, part, s2s.at[zs], s2r.at[zs], (ctx, 2 * ((y + k) % 4) + xh))

    def x_copies(zs):
        low = rows_of(zs, j, 0, 64)
        high = rows_of(zs, j, 64, 64)
        return (copy(low, low, s2s.at[zs], s3r.at[zs], x_up),
                copy(high, high, s2s.at[zs], s3r.at[zs], x_down))

    def core_copy(zs, member, send):
        part = rows_of(zs, member, 0, ROWS)
        return copy(part, part, send.at[zs], s4r.at[zs], core)

    def stage1(d):
        zs = z - d
        arrived(rows_of(zs, j, y * 32, 32), s1r.at[zs])
        for k in range(1, 4):
            y_copy(zs, k).start()

    def stage2(d, wait=True):
        zs = z - d
        if wait:
            arrived(rows_of(zs, j, 0, 96), s2r.at[zs])
        for each in x_copies(zs):
            each.start()
        core_copy(zs, j, s2s).start()

    def stage3(d):
        zs = z - d
        arrived(rows_of(zs, opp, 0, ROWS), s3r.at[zs])
        core_copy(zs, opp, s2s).start()

    def stage4(d):
        zs = z - d
        arrived(lat.at[zs, pl.ds(0, 2 * ROWS), :], s4r.at[zs])

    swap = copy(w_ref.at[pl.ds(al((1 - xh) * HALF, 16), HALF), :], ball.at[z, xh], sws, swr, over)

    def ring_up(u):
        part = ball.at[(z + NZ - u // 2) % NZ, (xh + u) % 2]
        return copy(part, part, brs, brr.at[u], z_up)

    def ring_down(u):
        part = ball.at[(z + u // 2) % NZ, (xh + u + u // 6) % 2]
        return copy(part, part, bls, blr.at[u], z_down)

    def pass_up(k):
        arrived(ball.at[(z + 7 - k // 2) % NZ, (xh + k) % 2], brr.at[k])

        @pl.when(k < 5)
        def _():
            ring_up(k + 2).start()

    def pass_down(k):
        arrived(ball.at[(z + 1 + k // 2) % NZ, (xh + k + k // 6) % 2], blr.at[k])

        @pl.when(k < 4)
        def _():
            ring_down(k + 2).start()

        @pl.when(k == 5)
        def _():
            ring_down(6).start()

    def forward(k):
        @pl.when(z < 4)
        def _():
            pass_down(k)
            pass_up(k)

        @pl.when(z >= 4)
        def _():
            pass_up(k)
            pass_down(k)

    def when_in(d, act):
        @pl.when(d <= z)
        def _():
            act(d)

    swap.start()
    stage2(0, wait=False)
    ring_up(0).start()
    ring_down(0).start()

    def absorb(h):
        lanes = slice(h * ROWS, (h + 1) * ROWS)
        qa = lax.dot_general(uk_ref[:, h * NOPE:(h + 1) * NOPE], q_ref[:, h * HD:h * HD + NOPE], NT,
                             preferred_element_type=jnp.float32)
        qt[:LATENT, lanes] = (qa * SCALE).astype(jnp.bfloat16)
        qr = q_ref[:, h * HD + NOPE:(h + 1) * HD].astype(jnp.float32) * SCALE
        qt[LATENT:LATENT + ROPE, lanes] = qr.T.astype(jnp.bfloat16)

    qt[LATENT + ROPE:, :] = jnp.zeros((WIDE - LATENT - ROPE, TOTAL), jnp.bfloat16)
    fetch[2].wait()
    fetch[3].wait()
    for h in range(HEADS):
        absorb(h)
    fetch[4].wait()
    uvt[...] = uv_ref[...].T
    for d in range(1, 4):
        when_in(d, stage1)
    stage3(0)
    arrived(ball.at[z, 1 - xh], swr)
    ring_up(1).start()
    ring_down(1).start()
    when_in(4, stage1)
    when_in(5, stage1)
    when_in(1, stage2)

    def visit(zs, first, chunk=None):
        block = lat[zs]
        turned = block[:, :LATENT].T

        def score(c):
            s = jnp.dot(block, qt[:, c * CHUNK:(c + 1) * CHUNK], preferred_element_type=jnp.float32)
            if first:
                row = j * ROWS + lax.broadcasted_iota(jnp.int32, s.shape, 1) % ROWS
                s = jnp.where(row >= lax.broadcasted_iota(jnp.int32, s.shape, 0), s, -jnp.inf)
            return s

        def rest(s, c):
            lanes = slice(c * CHUNK, (c + 1) * CHUNK)
            m_new = jnp.max(s, axis=0, keepdims=True)
            if not first:
                m_old = m_ref[:, lanes]
                m_new = jnp.maximum(m_old, m_new)
                alpha = jnp.exp2(m_old - m_new)
            p = jnp.exp2(s - m_new)
            total = jnp.sum(p, axis=0, keepdims=True)
            part = jnp.dot(turned, p.astype(jnp.bfloat16), preferred_element_type=jnp.float32)
            m_ref[:, lanes] = m_new
            if first:
                l_ref[:, lanes] = total
                acc[:, lanes] = part
            else:
                l_ref[:, lanes] = l_ref[:, lanes] * alpha + total
                acc[:, lanes] = acc[:, lanes] * alpha + part

        if chunk is None:
            s = score(0)
            later = score(1)
            rest(s, 0)
            rest(later, 1)
        else:
            rest(score(chunk), chunk)

    stage4(0)
    visit(z, True)
    when_in(2, stage2)
    when_in(6, stage1)
    when_in(3, stage2)
    when_in(1, stage3)
    forward(0)

    @pl.loop(1, z)
    def _(i):
        when_in(i + 1, stage3)
        when_in(i + 6, stage1)
        when_in(i + 3, stage2)
        stage4(i)
        visit(z - i, False)

        @pl.when(jnp.where(z >= 5, (i == 2) | (i == 4), i % 2 == 1))
        def _():
            forward((i + 1) // 2)

    def last_visit(c):
        @pl.when(z >= 1)
        def _():
            if c == 0:
                stage4(z)
            visit(0, False, c)

    done = 1 + jnp.minimum(z, 4) // 2

    def piece(across, member, c, start=0, count=PART):
        return abuf.at[across, pl.ds(c * PART + start, count), pl.ds(al(member * ROWS, ROWS), ROWS)]

    def a_sends(c):
        part = piece(xh, j, c)
        return (copy(part, part, axs, axr.at[c, 0], x_up),
                copy(part, part, axs, axr.at[c, 1], x_down),
                copy(part, part, axs, acr, core))

    def a_from_down(c):
        part, half = piece(down_xh, opp, c), piece(down_xh, opp, c, 0, PART // 2)
        return (copy(half, half, ars, arr.at[c], x_up),
                copy(part, part, ars, acr, core))

    def a_from_up(c):
        part, half = piece(up_xh, opp, c), piece(up_xh, opp, c, PART // 2, PART // 2)
        return (copy(half, half, ars, arr.at[c], x_down),
                copy(part, part, ars, acr, core))

    def a_across(c):
        part = piece(1 - xh, j, c)
        return copy(part, part, ars, acr, core)

    for c in range(4):
        if c % 2 == 0:
            last_visit(c // 2)
        for h in range(c * 2, c * 2 + 2):
            lanes = slice(h * ROWS, (h + 1) * ROWS)
            o = (acc[:, lanes] / l_ref[:, lanes]).astype(jnp.bfloat16)
            a = jnp.dot(uvt[h * NOPE:(h + 1) * NOPE, :], o, preferred_element_type=jnp.float32)
            abuf[xh, h * NOPE:(h + 1) * NOPE, mine] = a.astype(jnp.bfloat16)
        for each in a_sends(c):
            each.start()
        if c == 1:
            forward(done)
    for c in range(4):
        arrived(piece(down_xh, opp, c), axr.at[c, 0])
        for each in a_from_down(c):
            each.start()
        arrived(piece(up_xh, opp, c), axr.at[c, 1])
        for each in a_from_up(c):
            each.start()

    forward(done + 1)

    for c in range(4):
        arrived(piece(1 - xh, j, c), arr.at[c])
        a_across(c).start()
    forward(done + 2)
    arrived(abuf.at[0], acr)

    def home(s):
        far = (s + 1) // 2
        return (z + NZ + far * (1 - 2 * (s % 2))) % NZ

    def c_copy(s, t):
        return copy(cbuf.at[s, t], rbuf.at[s, y], cs, cr.at[s], (ctx, 2 * t + xh))

    def each_copy(s, act):
        for t in range(4):
            @pl.when(t != y)
            def _():
                act(c_copy(s, t))

    def multiply(slots):
        ct = None
        for across in range(2):
            blocks = [ball[home(s), across] for s in slots]
            rows = jnp.concatenate(blocks, axis=0) if len(blocks) > 1 else blocks[0]
            part = jnp.dot(rows, abuf[across], preferred_element_type=jnp.float32)
            ct = part if ct is None else ct + part
        ct = ct.astype(jnp.bfloat16)
        for r, s in enumerate(slots):
            for t in range(4):
                cbuf[s, t] = ct[r * HALF:(r + 1) * HALF, t * ROWS:(t + 1) * ROWS]
            each_copy(s, lambda each: each.start())

    spot = fin.at[pl.ds(al((2 * j + xh) * HALF, HALF), HALF), :]

    def f_copy(s):
        return copy(fsrc.at[s], spot, fs, fr, (base + y, home(s)))

    def is_here(s):
        return (y == j) & (home(s) == head)

    def gather(s):
        arrived(rbuf.at[s, pl.ds(0, 3)], cr.at[s])
        total = cbuf[s, y].astype(jnp.float32)
        for k in range(1, 4):
            total = total + rbuf[s, (y + k) % 4].astype(jnp.float32)
        fsrc[s] = total.astype(jnp.bfloat16)
        here = is_here(s)

        @pl.when(here)
        def _():
            spot[...] = fsrc[s]

        @pl.when(jnp.logical_not(here))
        def _():
            f_copy(s).start()

    def reach(k):
        @pl.when(k >= done + 3)
        def _():
            forward(k)

    multiply([0])

    @pl.loop(1, 4)
    def _(g):
        reach(2 * g - 2)
        reach(2 * g - 1)
        multiply([2 * g - 1, 2 * g])

        @pl.when(g == 3)
        def _():
            for s in range(3):
                gather(s)

    reach(6)
    multiply([7])

    @pl.loop(3, NZ)
    def _(s):
        gather(s)

    @pl.when(j == y)
    def _():
        arrived(fin.at[pl.ds(0, 7 * HALF), :], fr)

    @pl.when(j != y)
    def _():
        arrived(fin, fr)

    out_ref[...] = fin[...]

    for k in range(1, NZ):
        @pl.when(z + k < NZ)
        def _():
            z_copy(k).wait_send()

    @pl.loop(0, z + 1)
    def _(zs):
        @pl.when(zs < z)
        def _():
            left(lat.at[zs, pl.ds(0, 480), :], s2s.at[zs])

        @pl.when(zs == z)
        def _():
            left(lat.at[zs, pl.ds(0, 384), :], s2s.at[zs])

    swap.wait_send()

    left(ball.at[pl.ds(0, 7), 0], brs)
    left(ball.at[pl.ds(0, 7), 0], bls)

    left(abuf.at[0, pl.ds(0, 768), :], axs)
    left(abuf.at[0], ars)

    left(cbuf.at[:, pl.ds(0, 3)], cs)

    @pl.when(j == y)
    def _():
        left(fsrc.at[pl.ds(0, 7)], fs)

    @pl.when(j != y)
    def _():
        left(fsrc, fs)


def on_device(queries, compressed, latent_gain, w_uk, w_uv, w_out):
    dma = pltpu.SemaphoreType.DMA
    bf = jnp.bfloat16
    return pl.pallas_call(
        kernel,
        out_shape=jax.ShapeDtypeStruct((NZ * HALF, ROWS), bf),
        in_specs=[pl.BlockSpec(memory_space=pltpu.VMEM if n == 2 else pl.ANY) for n in range(6)],
        out_specs=pl.BlockSpec(memory_space=pltpu.VMEM),
        scratch_shapes=[
            pltpu.VMEM((ROWS, HEADS * HD), bf),
            pltpu.VMEM((LATENT + ROPE, ROWS), bf),
            pltpu.VMEM((LATENT, HEADS * NOPE), bf),
            pltpu.VMEM((LATENT, HEADS * NOPE), bf),
            pltpu.VMEM((2 * HALF, HEADS * NOPE), bf),
            dma((5,)),
            pltpu.VMEM((NZ, STRIP, WIDE), bf),
            pltpu.VMEM((NZ, 2, HALF, HEADS * NOPE), bf),
            pltpu.VMEM((WIDE, TOTAL), bf),
            pltpu.VMEM((HEADS * NOPE, LATENT), bf),
            pltpu.VMEM((1, TOTAL), jnp.float32),
            pltpu.VMEM((1, TOTAL), jnp.float32),
            pltpu.VMEM((LATENT, TOTAL), jnp.float32),
            pltpu.VMEM((2, HEADS * NOPE, STRIP), bf),
            pltpu.VMEM((NZ, 4, HALF, ROWS), bf),
            pltpu.VMEM((NZ, 4, HALF, ROWS), bf),
            pltpu.VMEM((NZ, HALF, ROWS), bf),
            pltpu.VMEM((NZ * HALF, ROWS), bf),
            dma((NZ,)), dma((NZ,)),
            dma((NZ,)), dma((NZ,)),
            dma((NZ,)), dma((NZ,)),
            dma, dma,
            dma, dma((7,)),
            dma, dma((7,)),
            dma, dma((4, 2)),
            dma, dma((4,)), dma,
            dma, dma((NZ,)),
            dma, dma,
        ],
        compiler_params=pltpu.CompilerParams(
            collective_id=0, has_side_effects=True, vmem_limit_bytes=56 * 1024 * 1024),
        name="layer",
    )(queries, compressed.T, latent_gain.reshape(1, LATENT), w_uk, w_uv, w_out.T).T


def solution(mesh):
    return jax.shard_map(
        on_device,
        mesh=mesh,
        in_specs=(
            P("ctx", "head"),
            P("ctx", None),
            P(),
            P(None, "head"),
            P(None, "head"),
            P("head", "ctx"),
        ),
        out_specs=P("ctx", "head"),
        check_vma=False,
    )
```
